512 devices in a mesh: gx: 32 (over y, x), gy: 16 (over z, core).
Axes of the slice: x: 4, y: 8, z: 8, core: 2. Of those that a mesh axis runs over, the one named last changes fastest.
Arguments:
- rhs: float32 [24, 256, 128, 128], P(None, 'gx', 'gy'), may hold values from -8 to 8
- shift: float32 [256, 128, 128], P('gx', 'gy'), may hold values from 0.05 to 2
- slots: int32 [32, 16], P('gx', 'gy'), may hold values from 0 to 15, each once within a row
- coarse_inverse: float32 [32, 16, 128, 2048], P('gx', 'gy'), may hold values from -16 to 16
Outputs:
- corrected: float32 [24, 256, 128, 128], P(None, 'gx', 'gy')
The draws below stay inside these ranges and needn't reach their ends.
Inputs may be any that keep to these rules, and one draw needn't show every extreme that they name: Each row of slots holds every number 0 to 15 once.
All inputs are finite; a program needn't handle non-finite values.
Results may differ from the reference program's by a relative error of at most 0.0001.
Values sent between devices are 32-bit elements; how exact they have to be, the bound alone decides.
No kernel may reach another device: no remote copies, remote signals or barrier semaphores. Data moves between devices by JAX's collectives and lax.ppermute only.
A program may use at most 64 MiB of HBM per device.

```python
import math
import jax
import jax.numpy as jnp
from jax import lax

CH = 24
CX = 8
CY = 8
NZ = 128
DEGREE = 3
SLABS = 32
POSITIONS = 16
NX = 256
NY = 128
LINE_CELLS = 2048


def draw_coarse_inverse(key, part):
    key = jax.random.fold_in(key, 11)
    first, second = jax.random.split(key)
    shape = (SLABS, POSITIONS, NZ, LINE_CELLS)
    offdiag = jnp.clip(jax.random.normal(first, shape, jnp.float32) * (5.6 / math.sqrt(LINE_CELLS)), -8.0, 8.0)
    diagonal = jax.random.uniform(second, shape[:3], jnp.float32, 4.8, 14.4)
    row_index = jnp.arange(POSITIONS)[:, None] * NZ + jnp.arange(NZ)[None, :]
    on_diag = row_index[None, :, :, None] == jnp.arange(LINE_CELLS)[None, None, None, :]
    return jnp.where(on_diag, diagonal[..., None], offdiag)


def block_scale(rng, shape, cuts, least, high):
    loudness, own = 1.0, jax.random.fold_in(rng, 6)
    for axis_at, shards_of in cuts:
        steps = jnp.exp(jax.random.uniform(jax.random.fold_in(own, axis_at), (shards_of,), jnp.float32, least / len(cuts), high / len(cuts)))
        loudness = loudness * jnp.repeat(steps, shape[axis_at] // shards_of).reshape([-1 if axis == axis_at else 1 for axis in range(len(shape))])
    return loudness


def gaussian(key, extent, scale, bound, shards=(), kind=jnp.bfloat16):
    drawn = jax.random.normal(key, extent, jnp.float32) * scale
    if len(shards) > 0:
        drawn = block_scale(key, extent, shards, -0.22, 0.18) * drawn
    return jnp.clip(drawn, min=-bound, max=bound).astype(kind)


def setup_inputs(seed: int = 0) -> dict:
    keys = jax.random.split(jax.random.key(seed), 5)
    return {
        "rhs": gaussian(keys[0], (CH, NX, NY, NZ), 1.0, 8.0, ((1, 32), (2, 16)), jnp.float32),
        "shift": jnp.clip(jnp.exp(math.log(2.0) - 3.6888794 * jax.random.uniform(keys[1], (NX, NY, NZ), jnp.float32) ** block_scale(keys[1], (NX, NY, NZ), ((0, 32), (1, 16)), -0.2, 0.2)), 0.05, 2.0),
        "slots": jax.vmap(lambda own: jax.random.permutation(own, POSITIONS))(jax.random.split(keys[2], SLABS)).reshape((SLABS, POSITIONS)).astype(jnp.int32),
        "coarse_inverse": draw_coarse_inverse(jax.random.fold_in(keys[4], 71), 0),
    }


THETA = 8.0
DELTA = 6.5


def restrict(v):
    xs, ys, zs = v.shape[-3:]
    return v.reshape(v.shape[:-3] + (xs // 2, 2, ys // 2, 2, zs)).mean(axis=(-4, -2))


def prolong(v):
    return jnp.repeat(jnp.repeat(v, 2, axis=-3), 2, axis=-2)


def operate(field, level_shift):
    padded = jnp.pad(field, 1)
    beside = padded[2:, 1:-1, 1:-1] + padded[:-2, 1:-1, 1:-1]
    beside = beside + padded[1:-1, 2:, 1:-1] + padded[1:-1, :-2, 1:-1]
    beside = beside + padded[1:-1, 1:-1, 2:] + padded[1:-1, 1:-1, :-2]
    return (6.0 + level_shift) * field - beside


def chebyshev(right, level_shift):
    sigma = THETA / DELTA
    rho = 1.0 / sigma
    step_dir = right / THETA
    iterate = step_dir
    for turn in range(DEGREE - 1):
        rho_new = 1.0 / (2.0 * sigma - rho)
        step_dir = rho_new * rho * step_dir + (2.0 * rho_new / DELTA) * (right - operate(iterate, level_shift))
        iterate = iterate + step_dir
        rho = rho_new
    return iterate


def reference(rhs, shift, slots, coarse_inverse):
    shifts = [shift, restrict(shift), restrict(restrict(shift))]
    places = (slots[:, :, None] == jnp.arange(POSITIONS, dtype=jnp.int32)[None, None, :]).astype(jnp.float32)
    high = lax.Precision.HIGHEST

    def one_channel(start):
        current = start
        iterates = []
        rights = []
        for level in range(3):
            iterate = chebyshev(current, shifts[level])
            leftover = current - operate(iterate, shifts[level])
            iterates.append(iterate)
            rights.append(current)
            current = restrict(leftover) if level < 2 else leftover
        blocks = current.reshape(SLABS, CX // 4, POSITIONS, CY // 4, NZ).mean(axis=(1, 3))
        ordered = jnp.einsum("sjm,sjk->smk", places, blocks, precision=high)
        flat = ordered.reshape(SLABS, LINE_CELLS)
        solved = jnp.einsum("smkn,sn->smk", coarse_inverse, flat, precision=high)
        back = jnp.einsum("sjm,smk->sjk", places, solved, precision=high)
        spread = jnp.broadcast_to(back[:, None, :, None, :], (SLABS, CX // 4, POSITIONS, CY // 4, NZ))
        upward = spread.reshape(NX // 4, NY // 4, NZ)
        for level in (2, 1, 0):
            iterate = iterates[level] + upward
            leftover = rights[level] - operate(iterate, shifts[level])
            iterate = iterate + chebyshev(leftover, shifts[level])
            upward = prolong(iterate)
        return iterate

    return lax.map(one_channel, rhs)
```

```python
import functools
import math

import jax
import jax.numpy as jnp
from jax import lax
from jax.experimental import pallas as pl
from jax.experimental.pallas import tpu as pltpu
from jax.sharding import PartitionSpec as P

THETA = 8.0
DELTA = 6.5
ROOTS = tuple(THETA + DELTA * math.cos(math.pi * (2 * k + 1) / 6) for k in range(3))
HALO = 3


def swap(x, axis, dist, odd):
    count = lax.axis_size(axis)
    pairs = []
    for i in range(count - dist):
        if (i // dist) % 2 == odd:
            pairs += [(i, i + dist), (i + dist, i)]
    return lax.ppermute(x, axis, pairs)


def parity(axis, dist):
    return lax.rem(lax.div(lax.axis_index(axis), dist), 2)


def swap_ends(low, high, axis, dist):
    even = parity(axis, dist) == 0
    first = swap(jnp.where(even, high, low), axis, dist, 0)
    second = swap(jnp.where(even, low, high), axis, dist, 1)
    return first, second


def in_order(first, second, axis, dist):
    even = parity(axis, dist) == 0
    return jnp.where(even, second, first), jnp.where(even, first, second)


def cells(x):
    return x.reshape((-1,) + x.shape[-2:])


def z_neighbours(v):
    lane = lax.broadcasted_iota(jnp.int32, v.shape, 1)
    below = jnp.where(lane == 0, 0.0, pltpu.roll(v, 1, 1))
    above = jnp.where(lane == v.shape[1] - 1, 0.0, pltpu.roll(v, v.shape[1] - 1, 1))
    return below + above


def inside(at, size):
    return jnp.where((at >= 0) & (at < size), 1.0, 0.0).astype(jnp.float32)


def beside(src, x, y):
    centre = src[x, y]
    total = (src[x - 1, y] + src[x + 1, y]) + (src[x, y - 1] + src[x, y + 1])
    return total + z_neighbours(centre), centre


def factor_cell(src, x, y, shift_row, root, mask):
    total, centre = beside(src, x, y)
    scale = mask * (1.0 / root)
    return (scale * ((root - 6.0) - shift_row)) * centre + scale * total


def factor(src, dst, shift, shift_at, size, root, masks):
    def row(x, carry):
        row_mask = masks(x, None)
        for y in range(size):
            shift_row = shift[x + shift_at, pl.ds(y + shift_at, 1), :]
            mask = row_mask * masks(None, y)
            dst[x, y] = factor_cell(src, x + 1, y + 1, shift_row, root, mask)
        return carry

    lax.fori_loop(0, size, row, 0)


def masks_of(where, reach, grid):
    def masks(x, y):
        if x is not None:
            return inside(where[0] + x - reach, grid[0])
        return inside(where[1] + y - reach, grid[1])

    return masks


def put_columns(dst, centre, pieces, where, rows, width, reach):
    def row(x, carry):
        for y in range(width):
            dst[x, reach + y] = centre[x, y]
        for ref, base, columns, dist, odd in pieces:
            gap = 0 if dist == 1 else reach - columns
            right, left = reach + width + gap, reach - columns - gap
            if odd:
                right, left = left, right
            at = jnp.where(where[1 + dist] == 0, right, left)
            for k in range(columns):
                dst[x, at + k] = ref[base + x * columns + k]
        return carry

    lax.fori_loop(0, rows, row, 0)


def down_kernel(n, grid, layout, where, rows, *refs):
    sides = refs[: len(layout)]
    shift, iterate, leftover, coarser, pad, one, two = refs[len(layout) :]
    pieces = [(ref,) + piece for ref, piece in zip(sides, layout)]
    put_columns(pad, rows, pieces, where, n + 2 * HALO, n, HALO)
    factor(pad, one, shift, 0, n + 4, ROOTS[0], masks_of(where, 2, grid))
    factor(one, two, shift, 1, n + 2, ROOTS[1], masks_of(where, 1, grid))

    def row(x, carry):
        for y in range(n):
            shift_row = shift[x + 2, pl.ds(y + 2, 1), :]
            leftover[x, y] = factor_cell(two, x + 1, y + 1, shift_row, ROOTS[2], 1.0)
            iterate[x, y] = (
                pad[x + 3, y + 3] * (1.0 / ROOTS[0])
                + one[x + 2, y + 2] * (1.0 / ROOTS[1])
                + two[x + 1, y + 1] * (1.0 / ROOTS[2])
            )
        return carry

    lax.fori_loop(0, n, row, 0)

    def coarse_row(x, carry):
        for y in range(n // 2):
            near = leftover[2 * x, 2 * y] + leftover[2 * x, 2 * y + 1]
            far = leftover[2 * x + 1, 2 * y] + leftover[2 * x + 1, 2 * y + 1]
            coarser[x, y] = 0.25 * (near + far)
        return carry

    lax.fori_loop(0, n // 2, coarse_row, 0)


def up_kernel(n, grid, layout, where, coarse_rows, *refs):
    half = n // 2
    sides = refs[: len(layout)]
    shift, iterate, leftover_rows, left_first, left_second, result, coarse, start, one = refs[len(layout) :]
    if layout[0] is None:
        for k in range(5):
            coarse[2, k] = coarse_rows[k]
            for ref, dist, odd in zip(sides, (1, 1, 2, 2), (0, 1, 0, 1)):
                ahead, behind = (2 - dist, 2 + dist) if odd else (2 + dist, 2 - dist)
                coarse[jnp.where(where[3 + dist] == 0, ahead, behind), k] = ref[k]
    else:
        put_columns(coarse, coarse_rows, [(ref,) + piece for ref, piece in zip(sides, layout)], where, half + 4, half, 2)
    put_columns(
        start, leftover_rows, [(left_first, where[6], 2, 1, 0), (left_second, where[6], 2, 1, 1)], where, n + 4, n, 2
    )
    outer = masks_of(where, 2, grid)

    def first_row(x, carry):
        row_mask = outer(x, None)
        here, before, after = (x + 2) // 2, (x + 1) // 2, (x + 3) // 2
        for y in range(n + 4):
            at, left, right = (y + 2) // 2, (y + 1) // 2, (y + 3) // 2
            centre = coarse[here, at]
            total = (coarse[before, at] + coarse[after, at]) + (coarse[here, left] + coarse[here, right])
            total = total + z_neighbours(centre)
            shift_row = shift[x, pl.ds(y, 1), :]
            mask = row_mask * outer(None, y)
            start[x, y] = mask * ((start[x, y] - (6.0 + shift_row) * centre) + total)
        return carry

    lax.fori_loop(0, n + 4, first_row, 0)
    factor(start, one, shift, 1, n + 2, ROOTS[0], masks_of(where, 1, grid))

    def row(x, carry):
        for y in range(n):
            shift_row = shift[x + 2, pl.ds(y + 2, 1), :]
            two = factor_cell(one, x + 1, y + 1, shift_row, ROOTS[1], 1.0)
            step = (
                start[x + 2, y + 2] * (1.0 / ROOTS[0]) + one[x + 1, y + 1] * (1.0 / ROOTS[1]) + two * (1.0 / ROOTS[2])
            )
            result[x, y] = (iterate[x, y] + coarse[x // 2 + 2, y // 2 + 2]) + step
        return carry

    lax.fori_loop(0, n, row, 0)


VMEM = pl.BlockSpec(memory_space=pltpu.VMEM)
SMEM = pl.BlockSpec(memory_space=pltpu.SMEM)


def call(kernel, where, operands, outs, scratch, name):
    tail = operands[0].shape[-2:]
    return pl.pallas_call(
        kernel,
        out_shape=[jax.ShapeDtypeStruct(out + tail, jnp.float32) for out in outs],
        in_specs=[SMEM] + [VMEM] * len(operands),
        out_specs=[VMEM] * len(outs),
        scratch_shapes=[pltpu.VMEM(own + tail, jnp.float32) for own in scratch],
        compiler_params=pltpu.CompilerParams(vmem_limit_bytes=32 * 1024 * 1024),
        name=name,
    )(where, *operands)


def place(n, offset=0):
    return jnp.stack(
        [
            lax.axis_index("gx") * n,
            lax.axis_index("gy") * n,
            parity("gy", 1),
            parity("gy", 2),
            parity("gx", 1),
            parity("gx", 2),
            jnp.int32(offset),
        ]
    ).astype(jnp.int32)


def grid_of(n):
    return (lax.axis_size("gx") * n, lax.axis_size("gy") * n)


def down(n, rows, sides, layout, shift):
    wide = n + 2 * HALO
    return call(
        functools.partial(down_kernel, n, grid_of(n), layout),
        place(n),
        [rows, *sides, shift],
        [(n, n), (n, n), (n // 2, n // 2)],
        [(wide, wide), (n + 4, n + 4), (n + 2, n + 2)],
        "down_%d" % n,
    )


def up(n, coarse_rows, sides, layout, shift, iterate, leftover_rows, left, offset):
    return call(
        functools.partial(up_kernel, n, grid_of(n), layout),
        place(n, offset),
        [coarse_rows, *sides, shift, iterate, leftover_rows, *left],
        [(n, n)],
        [(n // 2 + 4, n // 2 + 4), (n + 4, n + 4), (n + 2, n + 2)],
        "up_%d" % n,
    )[0]


def gx_rows(v, width):
    first, second = swap_ends(v[:width], v[v.shape[0] - width :], "gx", 1)
    before, after = in_order(first, second, "gx", 1)
    return jnp.concatenate([before, v, after], axis=0)


def gy_sides(rows, width):
    first, second = swap_ends(cells(rows[:, :width]), cells(rows[:, rows.shape[1] - width :]), "gy", 1)
    return [first, second]


BOTH = [(0, HALO, 1, 0), (0, HALO, 1, 1)]
BOTH_TWO = [(0, 2, 1, 0), (0, 2, 1, 1)]


def restrict_shift(v):
    xs, ys, zs = v.shape
    return v.reshape(xs // 2, 2, ys // 2, 2, zs).mean(axis=(1, 3))


def body(rhs, shift, slots, coarse_inverse):
    high = lax.Precision.HIGHEST
    right = jnp.transpose(rhs, (1, 2, 0, 3))
    n = right.shape[0]
    chans, depth = right.shape[2:]

    def with_shift(strip, block):
        flat = block.reshape(-1, depth)
        extra = -flat.shape[0] % chans
        flat = jnp.pad(flat, ((0, extra), (0, 0)))
        return jnp.concatenate([cells(strip), flat.reshape(-1, chans, depth)], axis=0)

    def shift_of(message, count, shape):
        flat = message[count:].reshape(-1, depth)
        return flat[: shape[0] * shape[1]].reshape(shape + (depth,))

    first, second = swap_ends(with_shift(right[:HALO], shift), with_shift(right[n - HALO :], shift), "gx", 1)
    before, after = in_order(first, second, "gx", 1)
    strip = HALO * n
    rows = jnp.concatenate(
        [before[:strip].reshape(HALO, n, chans, depth), right, after[:strip].reshape(HALO, n, chans, depth)], axis=0
    )
    shift_rows = jnp.concatenate([shift_of(before, strip, (n, n)), shift, shift_of(after, strip, (n, n))], axis=0)
    low, up_end = rows[:, :HALO], rows[:, n - HALO :]
    sides = swap_ends(with_shift(low, shift_rows), with_shift(up_end, shift_rows), "gy", 1)
    before, after = in_order(*sides, "gy", 1)
    strip = HALO * (n + 2 * HALO)
    shift_wide = jnp.concatenate(
        [shift_of(before, strip, (3 * n, n)), shift_rows, shift_of(after, strip, (3 * n, n))], axis=1
    )
    shift_one = restrict_shift(shift_wide)
    shift_two = restrict_shift(shift_one)
    shifts = [shift_wide[n - 2 : 2 * n + 2, n - 2 : 2 * n + 2], shift_one[2:-2, 2:-2], shift_two]

    x0, q0, b1 = down(n, rows, list(sides), BOTH, shifts[0])
    rows = gx_rows(b1, HALO)
    x1, q1, b2 = down(n // 2, rows, gy_sides(rows, HALO), BOTH, shifts[1])

    near = swap_ends(b2, b2, "gx", 1)
    far = swap_ends(b2[:1], b2[1:], "gx", 2)
    (before, after), (before_far, after_far) = in_order(*near, "gx", 1), in_order(*far, "gx", 2)
    rows = jnp.concatenate([before_far, before, b2, after, after_far], axis=0)
    near = swap_ends(cells(rows), cells(rows), "gy", 1)
    far = swap_ends(cells(rows[:, :1]), cells(rows[:, 1:]), "gy", 2)
    layout = [(0, 2, 1, 0), (0, 2, 1, 1), (0, 1, 2, 0), (0, 1, 2, 1)]
    x2, q2, b3 = down(n // 4, rows, [*near, *far], layout, shifts[2])

    lefts = [q0, q1, q2]
    low = jnp.concatenate([cells(q[:2]) for q in lefts], axis=0)
    up_end = jnp.concatenate([cells(q[-2:]) for q in lefts], axis=0)
    first, second = swap_ends(low, up_end, "gx", 1)
    before, after = in_order(first, second, "gx", 1)
    left_rows, at = [], 0
    for q in lefts:
        wide = 2 * q.shape[1]
        shape = (2,) + q.shape[1:]
        left_rows.append(
            jnp.concatenate([before[at : at + wide].reshape(shape), q, after[at : at + wide].reshape(shape)], axis=0)
        )
        at += wide
    low = jnp.concatenate([cells(q[:, :2]) for q in left_rows], axis=0)
    up_end = jnp.concatenate([cells(q[:, -2:]) for q in left_rows], axis=0)
    left_sides = swap_ends(low, up_end, "gy", 1)
    offsets = [0, 2 * (n + 4), 2 * (n + 4) + 2 * (n // 2 + 4)]

    count = lax.axis_size("gy")
    me = lax.axis_index("gy")
    slot = jnp.broadcast_to(slots.astype(jnp.float32), (8, depth))
    shares = lax.all_gather(jnp.concatenate([b3[0, 0], slot], axis=0)[None], "gy", axis=0, tiled=True)
    blocks = shares[:, :chans]
    slot_all = shares[:, chans, 0].astype(jnp.int32)
    places = (slot_all[None, :] == jnp.arange(count, dtype=jnp.int32)[:, None]).astype(jnp.float32)
    ordered = jnp.einsum("mj,jck->mck", places, blocks, precision=high)
    flat = ordered.transpose(1, 0, 2).reshape(chans, count * depth)
    solved = lax.dot_general(
        flat, coarse_inverse[0, 0], (((1,), (1,)), ((), ())), precision=high, preferred_element_type=jnp.float32
    )
    back = lax.all_gather(solved[None], "gy", axis=0, tiled=True)
    beside_me = me + jnp.arange(-2, 3, dtype=jnp.int32)
    wanted = (beside_me[:, None] == jnp.arange(count, dtype=jnp.int32)[None, :]).astype(jnp.float32)
    chosen = jnp.einsum("wj,mj->wm", wanted, places, precision=high)
    fix = jnp.einsum("wm,mck->wck", chosen, back, precision=high)
    lines = [*swap_ends(fix, fix, "gx", 1), *swap_ends(fix, fix, "gx", 2)]

    x2 = up(n // 4, fix, lines, [None] * 4, shifts[2], x2, left_rows[2], left_sides, offsets[2])
    rows = gx_rows(x2, 2)
    x1 = up(n // 2, rows, gy_sides(rows, 2), BOTH_TWO, shifts[1], x1, left_rows[1], left_sides, offsets[1])
    rows = gx_rows(x1, 2)
    x0 = up(n, rows, gy_sides(rows, 2), BOTH_TWO, shifts[0], x0, left_rows[0], left_sides, offsets[0])
    return jnp.transpose(x0, (2, 0, 1, 3))


def solution(mesh):
    return jax.shard_map(
        body,
        mesh=mesh,
        in_specs=(
            P(None, "gx", "gy", None),
            P("gx", "gy", None),
            P("gx", "gy"),
            P("gx", "gy", None, None),
        ),
        out_specs=P(None, "gx", "gy", None),
        check_vma=False,
    )
```

```python
import functools
import math

import jax
import jax.numpy as jnp
from jax import lax
from jax.experimental import pallas as pl
from jax.experimental.pallas import tpu as pltpu
from jax.sharding import PartitionSpec as P

THETA = 8.0
DELTA = 6.5
ROOTS = tuple(THETA + DELTA * math.cos(math.pi * (2 * k + 1) / 6) for k in range(3))
HALO = 3


def swap(x, axis, dist, odd):
    count = lax.axis_size(axis)
    pairs = []
    for i in range(count - dist):
        if (i // dist) % 2 == odd:
            pairs += [(i, i + dist), (i + dist, i)]
    return lax.ppermute(x, axis, pairs)


def parity(axis, dist):
    return lax.rem(lax.div(lax.axis_index(axis), dist), 2)


def swap_ends(at, low, high, axis, dist):
    even = at[axis]
    first = swap(jnp.where(even, high, low), axis, dist, 0)
    second = swap(jnp.where(even, low, high), axis, dist, 1)
    return first, second


def in_order(at, first, second, axis):
    even = at[axis]
    return jnp.where(even, second, first), jnp.where(even, first, second)


def cells(x):
    return x.reshape((-1,) + x.shape[-2:])


def z_neighbours(v):
    lane = lax.broadcasted_iota(jnp.int32, v.shape, 1)
    below = jnp.where(lane == 0, 0.0, pltpu.roll(v, 1, 1))
    above = jnp.where(lane == v.shape[1] - 1, 0.0, pltpu.roll(v, v.shape[1] - 1, 1))
    return below + above


def inside(at, size):
    return jnp.where((at >= 0) & (at < size), 1.0, 0.0).astype(jnp.float32)


def beside(src, x, y):
    centre = src[x, y]
    total = (src[x - 1, y] + src[x + 1, y]) + (src[x, y - 1] + src[x, y + 1])
    return total + z_neighbours(centre), centre


def factor_cell(src, x, y, shift_row, root, mask):
    total, centre = beside(src, x, y)
    scale = mask * (1.0 / root)
    return (scale * ((root - 6.0) - shift_row)) * centre + scale * total


def factor(src, dst, shift, shift_at, size, root, masks):
    def row(x, carry):
        row_mask = masks(x, None)
        for y in range(size[1]):
            shift_row = shift[x + shift_at[0], pl.ds(y + shift_at[1], 1), :]
            mask = row_mask * masks(None, y)
            dst[x, y] = factor_cell(src, x + 1, y + 1, shift_row, root, mask)
        return carry

    lax.fori_loop(0, size[0], row, 0)


def masks_of(first, reach, grid):
    def masks(x, y):
        if x is not None:
            return inside(first[0] + x - reach, grid[0])
        return inside(first[1] + y - reach, grid[1])

    return masks


def put_frame(dst, own, pieces, where, n, width):
    x_even, x_odd, y_even, y_odd, c_even, c_odd = pieces
    high = n + width
    rows = [jnp.where(where[3] == odd, high, 0) for odd in (0, 1)]
    columns = [jnp.where(where[2] == odd, high, 0) for odd in (0, 1)]

    def middle(x, carry):
        for y in range(n):
            dst[x + width, y + width] = own[x, y]
        for ref, at in ((y_even, columns[0]), (y_odd, columns[1])):
            for k in range(width):
                dst[x + width, at + k] = ref[x * width + k]
        return carry

    lax.fori_loop(0, n, middle, 0)

    def outer(x, carry):
        for ref, at in ((x_even, rows[0]), (x_odd, rows[1])):
            for y in range(n):
                dst[at + x, width + y] = ref[x * n + y]
        for ref, at in ((c_even, columns[0]), (c_odd, columns[1])):
            for k in range(width):
                dst[x, at + k] = ref[x * width + k]
                dst[high + x, at + k] = ref[(width + x) * width + k]
        return carry

    lax.fori_loop(0, width, outer, 0)


def put_columns(dst, centre, pieces, where, rows, width, reach):
    def row(x, carry):
        for y in range(width):
            dst[x, reach + y] = centre[x, y]
        for ref, base, odd in pieces:
            at = jnp.where(where[2] == odd, reach + width, 0)
            for k in range(reach):
                dst[x, at + k] = ref[base + x * reach + k]
        return carry

    lax.fori_loop(0, rows, row, 0)


def put_shift(wide, one, one_wide, two, own, pieces, where, n):
    x_even, x_odd, y_even, y_odd, c_even, c_odd = pieces
    chans = x_even.shape[1]
    strip, corner = HALO * n, 2 * HALO * HALO

    def line(ref, first, x):
        at = x * n
        return ref[first + at // chans, at % chans : at % chans + n, :]

    for odd, x_ref, y_ref, c_ref in ((0, x_even, y_even, c_even), (1, x_odd, y_odd, c_odd)):
        row = jnp.where(where[3] == odd, 2 * n, 0)
        column = pl.ds(pl.multiple_of(jnp.where(where[2] == odd, 2 * n, 0), n), n)
        for x in range(n):
            wide[row + x, n : 2 * n, :] = line(x_ref, strip, x)
            wide[n + x, column, :] = line(y_ref, strip, x)
            wide[x, column, :] = line(c_ref, corner, x)
            wide[2 * n + x, column, :] = line(c_ref, corner, n + x)
    for x in range(n):
        wide[n + x, n : 2 * n, :] = own[x]

    def halve(src, x, count):
        total = 0.0
        for k in range(4):
            total = total + src[2 * x + k // 2, pl.ds(k % 2, count, 2), :]
        return 0.25 * total

    half = n // 2
    for x in range(3 * half):
        row = halve(wide, x, 3 * half)
        one_wide[x, 0 : 3 * half, :] = row
        if half - 2 <= x < 2 * half + 2:
            one[x - half + 2] = row[half - 2 : 2 * half + 2]
    for x in range(3 * half // 2):
        two[x] = halve(one_wide, x, 3 * half // 2)


def down_body(size, grid, first, pad, shift, shift_at, iterate, leftover, coarser, one, two):
    nx, ny = size
    sx, sy = shift_at
    factor(pad, one, shift, (sx, sy), (nx + 4, ny + 4), ROOTS[0], masks_of(first, 2, grid))
    factor(one, two, shift, (sx + 1, sy + 1), (nx + 2, ny + 2), ROOTS[1], masks_of(first, 1, grid))

    def row(x, carry):
        for y in range(ny):
            shift_row = shift[x + 2 + sx, pl.ds(y + 2 + sy, 1), :]
            leftover[x, y] = factor_cell(two, x + 1, y + 1, shift_row, ROOTS[2], 1.0)
            iterate[x, y] = (
                pad[x + 3, y + 3] * (1.0 / ROOTS[0])
                + one[x + 2, y + 2] * (1.0 / ROOTS[1])
                + two[x + 1, y + 1] * (1.0 / ROOTS[2])
            )
        return carry

    lax.fori_loop(0, nx, row, 0)

    def coarse_row(x, carry):
        for y in range(ny // 2):
            near = leftover[2 * x, 2 * y] + leftover[2 * x, 2 * y + 1]
            far = leftover[2 * x + 1, 2 * y] + leftover[2 * x + 1, 2 * y + 1]
            coarser[x, y] = 0.25 * (near + far)
        return carry

    lax.fori_loop(0, nx // 2, coarse_row, 0)


def down_fine_kernel(n, grid, where, own, *refs):
    pieces, own_shift = refs[:6], refs[6]
    iterate, leftover, coarser, shift, shift_one, shift_two, one_wide, pad, one, two = refs[7:]
    put_frame(pad, own, pieces, where, n, HALO)
    put_shift(shift, shift_one, one_wide, shift_two, own_shift, pieces, where, n)
    first = (where[0] * n, where[1] * n)
    down_body((n, n), grid, first, pad, shift, (n - 2, n - 2), iterate, leftover, coarser, one, two)


def down_kernel(n, grid, where, own, *refs):
    pieces, shift = refs[:6], refs[6]
    iterate, leftover, coarser, pad, one, two = refs[7:]
    put_frame(pad, own, pieces, where, n, HALO)
    first = (where[0] * n, where[1] * n)
    down_body((n, n), grid, first, pad, shift, (0, 0), iterate, leftover, coarser, one, two)


def down_chip_kernel(size, grid, where, pad, shift, iterate, leftover, coarser, one, two):
    first = (where[0] * size[0], (where[1] - where[2]) * size[0])
    down_body(size, grid, first, pad, shift, (0, 0), iterate, leftover, coarser, one, two)


def solve_kernel(where, shares, inverse, solved, ordered):
    count, rows, depth = shares.shape
    chans = solved.shape[0]
    for m in range(count):
        block = jnp.zeros((chans, depth), jnp.float32)
        for j in range(count):
            block = jnp.where(shares[j, chans : chans + 1, :] == float(m), shares[j, 0:chans, :], block)
        ordered[:, m * depth : (m + 1) * depth] = block
    solved[...] = lax.dot_general(
        ordered[...],
        inverse[...],
        (((1,), (1,)), ((), ())),
        precision=lax.Precision.HIGHEST,
        preferred_element_type=jnp.float32,
    )


def pick_kernel(where, shares, back, picked):
    count, chans, depth = back.shape
    for k in range(picked.shape[0]):
        j = where[1] - where[2] + k - 2
        slot = shares[jnp.clip(j, 0, count - 1), pl.ds(chans, 1), :]
        slot = jnp.where((j >= 0) & (j < count), slot, -1.0)
        block = jnp.zeros((chans, depth), jnp.float32)
        for m in range(count):
            block = jnp.where(slot == float(m), back[m], block)
        picked[k] = block


def up_kernel(n, grid, shift_at, offset, pieces_count, where, coarse_own, *refs):
    half = n // 2
    sx, sy = shift_at
    pieces = refs[:pieces_count]
    shift, iterate, leftover_rows, left_even, left_odd, result, coarse, start, one = refs[pieces_count:]
    if pieces_count == 2:
        mine, others = pieces
        core, line, far = where[2], where[4], where[5]
        for k in range(5):
            coarse[2, k] = coarse_own[core + k]
            coarse[3 - 2 * line, k] = mine[core + k]
            coarse[1 + 2 * line, k] = others[core + k]
            coarse[4 * far, k] = mine[6 + core + k]
            coarse[4 - 4 * far, k] = others[6 + core + k]
    else:
        put_frame(coarse, coarse_own, pieces, where, half, 2)
    put_columns(start, leftover_rows, [(left_even, offset, 0), (left_odd, offset, 1)], where, n + 4, n, 2)
    first = (where[0] * n, where[1] * n)
    outer = masks_of(first, 2, grid)

    def first_row(x, carry):
        row_mask = outer(x, None)
        here, before, after = (x + 2) // 2, (x + 1) // 2, (x + 3) // 2
        for y in range(n + 4):
            at, left, right = (y + 2) // 2, (y + 1) // 2, (y + 3) // 2
            centre = coarse[here, at]
            total = (coarse[before, at] + coarse[after, at]) + (coarse[here, left] + coarse[here, right])
            total = total + z_neighbours(centre)
            shift_row = shift[x + sx, pl.ds(y + sy, 1), :]
            mask = row_mask * outer(None, y)
            start[x, y] = mask * ((start[x, y] - (6.0 + shift_row) * centre) + total)
        return carry

    lax.fori_loop(0, n + 4, first_row, 0)
    factor(start, one, shift, (sx + 1, sy + 1), (n + 2, n + 2), ROOTS[0], masks_of(first, 1, grid))

    def row(x, carry):
        for y in range(n):
            shift_row = shift[x + 2 + sx, pl.ds(y + 2 + sy, 1), :]
            two = factor_cell(one, x + 1, y + 1, shift_row, ROOTS[1], 1.0)
            step = (
                start[x + 2, y + 2] * (1.0 / ROOTS[0]) + one[x + 1, y + 1] * (1.0 / ROOTS[1]) + two * (1.0 / ROOTS[2])
            )
            result[x, y] = (iterate[x, y] + coarse[x // 2 + 2, y // 2 + 2]) + step
        return carry

    lax.fori_loop(0, n, row, 0)


VMEM = pl.BlockSpec(memory_space=pltpu.VMEM)
SMEM = pl.BlockSpec(memory_space=pltpu.SMEM)


def call(kernel, where, operands, outs, scratch, name):
    return pl.pallas_call(
        kernel,
        out_shape=[jax.ShapeDtypeStruct(out, jnp.float32) for out in outs],
        in_specs=[SMEM] + [VMEM] * len(operands),
        out_specs=[VMEM] * len(outs),
        scratch_shapes=[pltpu.VMEM(own, jnp.float32) for own in scratch],
        compiler_params=pltpu.CompilerParams(vmem_limit_bytes=12 * 1024 * 1024),
        name=name,
    )(where, *operands)


def place():
    core = parity("gy", 1)
    line, far = parity("gx", 1), parity("gx", 2)
    numbers = [lax.axis_index("gx"), lax.axis_index("gy"), core, line, line ^ core, far ^ core]
    where = jnp.stack(numbers + [jnp.zeros_like(core)] * 2).astype(jnp.int32)
    sides = {
        "gx": line == 0,
        "gy": core == 0,
        "line": line == core,
        "far": far != core,
        "chip": parity("gy", 2) == core,
    }
    return where, sides


def grid_of(n):
    return (lax.axis_size("gx") * n, lax.axis_size("gy") * n)


def up(n, where, coarse_own, pieces, shift, shift_at, iterate, leftover_rows, left, offset):
    tail = iterate.shape[-2:]
    return call(
        functools.partial(up_kernel, n, grid_of(n), shift_at, offset, len(pieces)),
        where,
        [coarse_own, *pieces, shift, iterate, leftover_rows, *left],
        [(n, n) + tail],
        [(n // 2 + 4, n // 2 + 4) + tail, (n + 4, n + 4) + tail, (n + 2, n + 2) + tail],
        "up_%d" % n,
    )[0]


def frame(at, v, width, blocks=None):
    n = v.shape[0]
    tail = v.shape[-2:]

    def message(strip, rows):
        flat = cells(strip)
        if rows is None:
            return flat
        rows = rows.reshape(-1, tail[1])
        rows = jnp.pad(rows, ((0, -rows.shape[0] % tail[0]), (0, 0)))
        return jnp.concatenate([flat, rows.reshape((-1,) + tail)], axis=0)

    def rows_of(piece):
        flat = piece[width * n :].reshape(-1, tail[1])[: blocks.shape[0] * blocks.shape[1]]
        return flat.reshape(blocks.shape)

    x_pieces = swap_ends(at, message(v[:width], blocks), message(v[n - width :], blocks), "gx", 1)
    y_pieces = swap_ends(at, message(v[:, :width], blocks), message(v[:, n - width :], blocks), "gy", 1)
    x_pieces, y_pieces = lax.optimization_barrier((x_pieces, y_pieces))
    sides = in_order(at, *x_pieces, "gx")
    strips = [side[: width * n].reshape((width, n) + tail) for side in sides]
    beyond = None if blocks is None else jnp.concatenate([rows_of(side) for side in sides], axis=0)
    low = jnp.concatenate([strip[:, :width] for strip in strips], axis=0)
    high = jnp.concatenate([strip[:, n - width :] for strip in strips], axis=0)
    corners = swap_ends(at, message(low, beyond), message(high, beyond), "gy", 1)
    return [*x_pieces, *y_pieces, *corners]


def by_core(x, swaps):
    lines, blocks = lax.axis_size("gx"), lax.axis_size("gy")
    pairs = []
    for j in range(blocks):
        dist, odd = swaps[j % 2]
        for i in range(lines - dist):
            if (i // dist) % 2 == odd:
                pairs += [(i * blocks + j, (i + dist) * blocks + j), ((i + dist) * blocks + j, i * blocks + j)]
    return lax.ppermute(x, ("gx", "gy"), pairs)


def to_core(x):
    return swap(x, "gy", 1, 0)


def lines_around(at, near, low, high):
    first = by_core(near, [(1, 0), (1, 1)])
    second = by_core(jnp.where(at["far"], high, low), [(2, 1), (2, 0)])
    mine = jnp.concatenate([cells(first), cells(second)], axis=0)
    return mine, to_core(mine)


def body(rhs, shift, slots, coarse_inverse):
    where, at = place()
    where, at, rhs = lax.optimization_barrier((where, at, rhs))
    right = jnp.transpose(rhs, (1, 2, 0, 3))
    n = right.shape[0]
    tail = chans, depth = right.shape[2:]
    half, size = n // 2, n // 4

    x0, q0, b1, shift_wide, shift_one, shift_two = call(
        functools.partial(down_fine_kernel, n, grid_of(n)),
        where,
        [right, *frame(at, right, HALO, shift), shift],
        [
            (n, n) + tail,
            (n, n) + tail,
            (half, half) + tail,
            (3 * n, 3 * n, depth),
            (half + 4, half + 4, depth),
            (3 * size, 3 * size, depth),
        ],
        [(3 * half, 2 * n, depth), (n + 6, n + 6) + tail, (n + 4, n + 4) + tail, (n + 2, n + 2) + tail],
        "down_fine",
    )
    x1, q1, b2 = call(
        functools.partial(down_kernel, half, grid_of(half)),
        where,
        [b1, *frame(at, b1, HALO), shift_one],
        [(half, half) + tail, (half, half) + tail, (size, size) + tail],
        [(half + 6, half + 6) + tail, (half + 4, half + 4) + tail, (half + 2, half + 2) + tail],
        "down_middle",
    )

    first_core = at["gy"]
    edge = jnp.where(first_core, shift_two[:, : 2 * size], shift_two[:, size:])
    edge_rows = edge.shape[0] * edge.shape[1]
    spare = -edge_rows % chans
    message = jnp.concatenate(
        [cells(b2), jnp.pad(edge.reshape(-1, depth), ((0, spare), (0, 0))).reshape(-1, chans, depth)], axis=0
    )
    other = to_core(message)
    edge = other[size * size :].reshape(-1, depth)[:edge_rows].reshape(edge.shape)
    other = other[: size * size].reshape(b2.shape)
    chip = jnp.concatenate([jnp.where(first_core, b2, other), jnp.where(first_core, other, b2)], axis=1)
    mine, others = lines_around(at, chip, chip[:1], chip[1:])
    near, wide = 2 * size * size, (1, 2 * size, chans, depth)
    mine_first, other_first = mine[:near].reshape(chip.shape), others[:near].reshape(chip.shape)
    mine_far, other_far = mine[near:].reshape(wide), others[near:].reshape(wide)
    rows = jnp.concatenate(
        [
            jnp.where(at["far"], other_far, mine_far),
            jnp.where(at["line"], other_first, mine_first),
            chip,
            jnp.where(at["line"], mine_first, other_first),
            jnp.where(at["far"], mine_far, other_far),
        ],
        axis=0,
    )
    blocks = lax.axis_size("gy")
    pairs = []
    for j in range(blocks - 2):
        if (j // 2) % 2 == j % 2:
            pairs += [(j, j + 2), (j + 2, j)]
    mine = lax.ppermute(jnp.where(at["chip"], rows[1:-1, 1:], rows[1:-1, :-1]), "gy", pairs)
    others = to_core(mine)
    ends = [jnp.where(at["chip"], others, mine), jnp.where(at["chip"], mine, others)]
    ends = [jnp.pad(end, ((1, 1), (0, 0), (0, 0), (0, 0))) for end in ends]
    pad = jnp.concatenate([ends[0], rows, ends[1]], axis=1)
    chip_shift = jnp.where(
        first_core,
        jnp.concatenate([shift_two[:, : 2 * size], edge], axis=1),
        jnp.concatenate([edge, shift_two[:, size:]], axis=1),
    )
    x2, q2, b3 = call(
        functools.partial(down_chip_kernel, (size, 2 * size), grid_of(size)),
        where,
        [pad, chip_shift],
        [(size, 2 * size) + tail, (size, 2 * size) + tail, (1, 2) + tail],
        [(size + 4, 2 * size + 4) + tail, (size + 2, 2 * size + 2) + tail],
        "down_chip",
    )
    x2, q2 = [jnp.where(first_core, v[:, :size], v[:, size:]) for v in (x2, q2)]
    b3 = jnp.where(first_core, b3[0, 0], b3[0, 1])

    lefts = [q0, q1, q2]
    low = jnp.concatenate([cells(q[:2]) for q in lefts], axis=0)
    high = jnp.concatenate([cells(q[-2:]) for q in lefts], axis=0)
    left_ends = swap_ends(at, low, high, "gx", 1)

    slot = jnp.broadcast_to(slots.astype(jnp.float32), (8, depth))
    shares = lax.all_gather(jnp.concatenate([b3, slot], axis=0)[None], "gy", axis=0, tiled=True)
    left_ends, shares = lax.optimization_barrier((left_ends, shares))
    before, after = in_order(at, *left_ends, "gx")
    left_rows, done = [], 0
    for q in lefts:
        strip = 2 * q.shape[1]
        shape = (2,) + q.shape[1:]
        ends = [side[done : done + strip].reshape(shape) for side in (before, after)]
        left_rows.append(jnp.concatenate([ends[0], q, ends[1]], axis=0))
        done += strip
    low = jnp.concatenate([cells(q[:, :2]) for q in left_rows], axis=0)
    high = jnp.concatenate([cells(q[:, -2:]) for q in left_rows], axis=0)
    left_sides = swap_ends(at, low, high, "gy", 1)
    offsets = [0, 2 * (n + 4), 2 * (n + 4) + 2 * (half + 4)]

    solved = call(
        solve_kernel, where, [shares, coarse_inverse[0, 0]], [tail], [(chans, blocks * depth)], "solve"
    )[0]
    back = lax.all_gather(solved[None], "gy", axis=0, tiled=True)
    fix = call(pick_kernel, where, [shares, back], [(6,) + tail], [], "pick")[0]
    lines = lines_around(at, fix, fix, fix)

    x2 = up(size, where, fix, lines, shift_two, (0, 0), x2, left_rows[2], left_sides, offsets[2])
    x1 = up(half, where, x2, frame(at, x2, 2), shift_one, (0, 0), x1, left_rows[1], left_sides, offsets[1])
    x0 = up(n, where, x1, frame(at, x1, 2), shift_wide, (n - 2, n - 2), x0, left_rows[0], left_sides, offsets[0])
    return jnp.transpose(x0, (2, 0, 1, 3))


def solution(mesh):
    return jax.shard_map(
        body,
        mesh=mesh,
        in_specs=(
            P(None, "gx", "gy", None),
            P("gx", "gy", None),
            P("gx", "gy"),
            P("gx", "gy", None, None),
        ),
        out_specs=P(None, "gx", "gy", None),
        check_vma=False,
    )
```

```python
import functools
import math

import jax
import jax.numpy as jnp
from jax import lax
from jax.experimental import pallas as pl
from jax.experimental.pallas import tpu as pltpu
from jax.sharding import PartitionSpec as P

THETA = 8.0
DELTA = 6.5
ROOTS = tuple(THETA + DELTA * math.cos(math.pi * (2 * k + 1) / 6) for k in range(3))
HALO = 3


def swap(x, axis, dist, odd):
    count = lax.axis_size(axis)
    pairs = []
    for i in range(count - dist):
        if (i // dist) % 2 == odd:
            pairs += [(i, i + dist), (i + dist, i)]
    return lax.ppermute(x, axis, pairs)


def parity(axis, dist):
    return lax.rem(lax.div(lax.axis_index(axis), dist), 2)


def swap_ends(at, low, high, axis, dist):
    even = at[axis]
    first = swap(jnp.where(even, high, low), axis, dist, 0)
    second = swap(jnp.where(even, low, high), axis, dist, 1)
    return first, second


def in_order(at, first, second, axis):
    even = at[axis]
    return jnp.where(even, second, first), jnp.where(even, first, second)


def cells(x):
    return x.reshape((-1,) + x.shape[-2:])


def z_neighbours(v):
    lane = lax.broadcasted_iota(jnp.int32, v.shape, 1)
    below = jnp.where(lane == 0, 0.0, pltpu.roll(v, 1, 1))
    above = jnp.where(lane == v.shape[1] - 1, 0.0, pltpu.roll(v, v.shape[1] - 1, 1))
    return below + above


def inside(at, size):
    return jnp.where((at >= 0) & (at < size), 1.0, 0.0).astype(jnp.float32)


def beside(src, x, y):
    centre = src[x, y]
    total = (src[x - 1, y] + src[x + 1, y]) + (src[x, y - 1] + src[x, y + 1])
    return total + z_neighbours(centre), centre


def factor_cell(src, x, y, shift_row, root, mask):
    total, centre = beside(src, x, y)
    scale = mask * (1.0 / root)
    return (scale * ((root - 6.0) - shift_row)) * centre + scale * total


def each_row(count, row):
    if count <= 4:
        for x in range(count):
            row(x)
        return

    def pair(step, carry):
        row(2 * step)
        row(2 * step + 1)
        return carry

    lax.fori_loop(0, count // 2, pair, 0)


def factor(src, dst, shift, shift_at, size, root, masks):
    def row(x):
        row_mask = masks(x, None)
        for y in range(size[1]):
            shift_row = shift[x + shift_at[0], pl.ds(y + shift_at[1], 1), :]
            mask = row_mask * masks(None, y)
            dst[x, y] = factor_cell(src, x + 1, y + 1, shift_row, root, mask)

    each_row(size[0], row)


def masks_of(first, reach, grid):
    def masks(x, y):
        if x is not None:
            return inside(first[0] + x - reach, grid[0])
        return inside(first[1] + y - reach, grid[1])

    return masks


def put_frame(dst, own, pieces, where, n, width):
    x_even, x_odd, y_even, y_odd = pieces
    high = n + width
    rows = [jnp.where(where[3] == odd, high, 0) for odd in (0, 1)]
    columns = [jnp.where(where[2] == odd, high, 0) for odd in (0, 1)]

    def middle(x):
        for y in range(n):
            dst[x + width, y + width] = own[x, y]

    def outer(x):
        for ref, at in ((x_even, rows[0]), (x_odd, rows[1])):
            for y in range(n):
                dst[at + x, width + y] = ref[x * n + y]

    def beside(x):
        for ref, at in ((y_even, columns[0]), (y_odd, columns[1])):
            for k in range(width):
                dst[x, at + k] = ref[x * width + k]

    each_row(n, middle)
    for x in range(width):
        outer(x)
    each_row(n + 2 * width, beside)


def put_columns(dst, centre, pieces, where, rows, width, reach):
    def row(x):
        for y in range(width):
            dst[x, reach + y] = centre[x, y]
        for ref, base, odd in pieces:
            at = jnp.where(where[2] == odd, reach + width, 0)
            for k in range(reach):
                dst[x, at + k] = ref[base + x * reach + k]

    each_row(rows, row)


def put_shift(wide, one, one_wide, two, own, pieces, where, n):
    x_even, x_odd, y_even, y_odd = pieces
    chans = x_even.shape[1]
    strip, side = HALO * n, HALO * (n + 2 * HALO)

    def line(ref, first, x):
        at = x * n
        return ref[first + at // chans, at % chans : at % chans + n, :]

    for odd, x_ref, y_ref in ((0, x_even, y_even), (1, x_odd, y_odd)):
        row = jnp.where(where[3] == odd, 2 * n, 0)
        column = pl.ds(pl.multiple_of(jnp.where(where[2] == odd, 2 * n, 0), n), n)
        for x in range(n):
            wide[row + x, n : 2 * n, :] = line(x_ref, strip, x)
        for x in range(3 * n):
            wide[x, column, :] = line(y_ref, side, x)
    for x in range(n):
        wide[n + x, n : 2 * n, :] = own[x]

    def halve(src, x, count):
        total = 0.0
        for k in range(4):
            total = total + src[2 * x + k // 2, pl.ds(k % 2, count, 2), :]
        return 0.25 * total

    half = n // 2
    for x in range(3 * half):
        row = halve(wide, x, 3 * half)
        one_wide[x, 0 : 3 * half, :] = row
        if half - 2 <= x < 2 * half + 2:
            one[x - half + 2] = row[half - 2 : 2 * half + 2]
    for x in range(3 * half // 2):
        two[x] = halve(one_wide, x, 3 * half // 2)


def down_body(size, grid, first, pad, shift, shift_at, iterate, leftover, coarser, one, two):
    nx, ny = size
    sx, sy = shift_at
    factor(pad, one, shift, (sx, sy), (nx + 4, ny + 4), ROOTS[0], masks_of(first, 2, grid))
    factor(one, two, shift, (sx + 1, sy + 1), (nx + 2, ny + 2), ROOTS[1], masks_of(first, 1, grid))

    def row(x):
        for y in range(ny):
            shift_row = shift[x + 2 + sx, pl.ds(y + 2 + sy, 1), :]
            leftover[x, y] = factor_cell(two, x + 1, y + 1, shift_row, ROOTS[2], 1.0)
            iterate[x, y] = (
                pad[x + 3, y + 3] * (1.0 / ROOTS[0])
                + one[x + 2, y + 2] * (1.0 / ROOTS[1])
                + two[x + 1, y + 1] * (1.0 / ROOTS[2])
            )

    each_row(nx, row)

    def coarse_row(x):
        for y in range(ny // 2):
            near = leftover[2 * x, 2 * y] + leftover[2 * x, 2 * y + 1]
            far = leftover[2 * x + 1, 2 * y] + leftover[2 * x + 1, 2 * y + 1]
            coarser[x, y] = 0.25 * (near + far)

    each_row(nx // 2, coarse_row)


def down_fine_kernel(n, grid, where, own, *refs):
    pieces, own_shift = refs[:4], refs[4]
    iterate, leftover, coarser, shift, shift_one, shift_two, one_wide, pad, one, two = refs[5:]
    put_frame(pad, own, pieces, where, n, HALO)
    put_shift(shift, shift_one, one_wide, shift_two, own_shift, pieces, where, n)
    first = (where[0] * n, where[1] * n)
    down_body((n, n), grid, first, pad, shift, (n - 2, n - 2), iterate, leftover, coarser, one, two)


def down_kernel(n, grid, where, own, *refs):
    pieces, shift = refs[:4], refs[4]
    iterate, leftover, coarser, pad, one, two = refs[5:]
    put_frame(pad, own, pieces, where, n, HALO)
    first = (where[0] * n, where[1] * n)
    down_body((n, n), grid, first, pad, shift, (0, 0), iterate, leftover, coarser, one, two)


def down_chip_kernel(size, grid, where, pad, shift, iterate, leftover, coarser, one, two):
    first = (where[0] * size[0], (where[1] - where[2]) * size[0])
    down_body(size, grid, first, pad, shift, (0, 0), iterate, leftover, coarser, one, two)


def solve_kernel(where, shares, inverse, solved, ordered):
    chips, _, depth = shares.shape
    chans = solved.shape[0]
    count = 2 * chips
    for m in range(count):
        block = jnp.zeros((chans, depth), jnp.float32)
        for j in range(count):
            slot = shares[j // 2, 2 * chans + 8 * (j % 2) : 2 * chans + 8 * (j % 2) + 1, :]
            block = jnp.where(slot == float(m), shares[j // 2, j % 2 * chans : (j % 2 + 1) * chans, :], block)
        ordered[:, m * depth : (m + 1) * depth] = block
    solved[...] = lax.dot_general(
        ordered[...],
        inverse[...],
        (((1,), (1,)), ((), ())),
        precision=lax.Precision.HIGHEST,
        preferred_element_type=jnp.float32,
    )


def pick_kernel(where, shares, back, picked):
    chips, rows, depth = back.shape
    chans = rows // 2
    for k in range(picked.shape[0]):
        j = where[1] - where[2] + k - 2
        chip = jnp.clip(where[6] + k // 2 - 1, 0, chips - 1)
        slot = shares[chip, pl.ds(2 * chans + 8 * (k % 2), 1), :]
        slot = jnp.where((j >= 0) & (j < 2 * chips), slot, -1.0)
        block = jnp.zeros((chans, depth), jnp.float32)
        for m in range(2 * chips):
            block = jnp.where(slot == float(m), back[m // 2, m % 2 * chans : (m % 2 + 1) * chans, :], block)
        picked[k] = block


def up_kernel(n, grid, shift_at, offset, pieces_count, where, coarse_own, *refs):
    half = n // 2
    sx, sy = shift_at
    pieces = refs[:pieces_count]
    shift, iterate, leftover_rows, left_even, left_odd, result, coarse, start, one = refs[pieces_count:]
    if pieces_count == 2:
        mine, others = pieces
        core, line, far = where[2], where[4], where[5]
        for k in range(5):
            coarse[2, k] = coarse_own[core + k]
            coarse[3 - 2 * line, k] = mine[core + k]
            coarse[1 + 2 * line, k] = others[core + k]
            coarse[4 * far, k] = mine[6 + core + k]
            coarse[4 - 4 * far, k] = others[6 + core + k]
    else:
        put_frame(coarse, coarse_own, pieces, where, half, 2)
    put_columns(start, leftover_rows, [(left_even, offset, 0), (left_odd, offset, 1)], where, n + 4, n, 2)
    first = (where[0] * n, where[1] * n)
    outer = masks_of(first, 2, grid)

    def first_row(x):
        row_mask = outer(x, None)
        here, before, after = (x + 2) // 2, (x + 1) // 2, (x + 3) // 2
        for y in range(n + 4):
            at, left, right = (y + 2) // 2, (y + 1) // 2, (y + 3) // 2
            centre = coarse[here, at]
            total = (coarse[before, at] + coarse[after, at]) + (coarse[here, left] + coarse[here, right])
            total = total + z_neighbours(centre)
            shift_row = shift[x + sx, pl.ds(y + sy, 1), :]
            mask = row_mask * outer(None, y)
            start[x, y] = mask * ((start[x, y] - (6.0 + shift_row) * centre) + total)

    each_row(n + 4, first_row)
    factor(start, one, shift, (sx + 1, sy + 1), (n + 2, n + 2), ROOTS[0], masks_of(first, 1, grid))

    def row(x):
        for y in range(n):
            shift_row = shift[x + 2 + sx, pl.ds(y + 2 + sy, 1), :]
            two = factor_cell(one, x + 1, y + 1, shift_row, ROOTS[1], 1.0)
            step = (
                start[x + 2, y + 2] * (1.0 / ROOTS[0]) + one[x + 1, y + 1] * (1.0 / ROOTS[1]) + two * (1.0 / ROOTS[2])
            )
            result[x, y] = (iterate[x, y] + coarse[x // 2 + 2, y // 2 + 2]) + step

    each_row(n, row)


VMEM = pl.BlockSpec(memory_space=pltpu.VMEM)
SMEM = pl.BlockSpec(memory_space=pltpu.SMEM)


def call(kernel, where, operands, outs, scratch, name):
    return pl.pallas_call(
        kernel,
        out_shape=[jax.ShapeDtypeStruct(out, jnp.float32) for out in outs],
        in_specs=[SMEM] + [VMEM] * len(operands),
        out_specs=[VMEM] * len(outs),
        scratch_shapes=[pltpu.VMEM(own, jnp.float32) for own in scratch],
        compiler_params=pltpu.CompilerParams(vmem_limit_bytes=12 * 1024 * 1024),
        name=name,
    )(where, *operands)


def place():
    core = parity("gy", 1)
    line, far = parity("gx", 1), parity("gx", 2)
    numbers = [lax.axis_index("gx"), lax.axis_index("gy"), core, line, line ^ core, far ^ core]
    numbers += [lax.div(lax.axis_index("gy"), 2), jnp.zeros_like(core)]
    where = jnp.stack(numbers).astype(jnp.int32)
    sides = {
        "gx": line == 0,
        "gy": core == 0,
        "line": line == core,
        "far": far != core,
        "chip": parity("gy", 2) == core,
    }
    return where, sides


def grid_of(n):
    return (lax.axis_size("gx") * n, lax.axis_size("gy") * n)


def up(n, where, coarse_own, pieces, shift, shift_at, iterate, leftover_rows, left, offset):
    tail = iterate.shape[-2:]
    return call(
        functools.partial(up_kernel, n, grid_of(n), shift_at, offset, len(pieces)),
        where,
        [coarse_own, *pieces, shift, iterate, leftover_rows, *left],
        [(n, n) + tail],
        [(n // 2 + 4, n // 2 + 4) + tail, (n + 4, n + 4) + tail, (n + 2, n + 2) + tail],
        "up_%d" % n,
    )[0]


def frame(at, v, width, blocks=None):
    n = v.shape[0]
    tail = v.shape[-2:]

    def message(strip, rows):
        flat = cells(strip)
        if rows is None:
            return flat
        rows = rows.reshape(-1, tail[1])
        rows = jnp.pad(rows, ((0, -rows.shape[0] % tail[0]), (0, 0)))
        return jnp.concatenate([flat, rows.reshape((-1,) + tail)], axis=0)

    def rows_of(piece):
        flat = piece[width * n :].reshape(-1, tail[1])[: blocks.shape[0] * blocks.shape[1]]
        return flat.reshape(blocks.shape)

    x_pieces = swap_ends(at, message(v[:width], blocks), message(v[n - width :], blocks), "gx", 1)
    sides = in_order(at, *x_pieces, "gx")
    strips = [side[: width * n].reshape((width, n) + tail) for side in sides]
    rows = None
    if blocks is not None:
        rows = jnp.concatenate([rows_of(sides[0]), blocks, rows_of(sides[1])], axis=0)
    low = jnp.concatenate([strips[0][:, :width], v[:, :width], strips[1][:, :width]], axis=0)
    high = jnp.concatenate([strips[0][:, n - width :], v[:, n - width :], strips[1][:, n - width :]], axis=0)
    return [*x_pieces, *swap_ends(at, message(low, rows), message(high, rows), "gy", 1)]


def by_core(x, swaps):
    lines, blocks = lax.axis_size("gx"), lax.axis_size("gy")
    pairs = []
    for j in range(blocks):
        dist, odd = swaps[j % 2]
        for i in range(lines - dist):
            if (i // dist) % 2 == odd:
                pairs += [(i * blocks + j, (i + dist) * blocks + j), ((i + dist) * blocks + j, i * blocks + j)]
    return lax.ppermute(x, ("gx", "gy"), pairs)


def to_core(x):
    return swap(x, "gy", 1, 0)


def lines_around(at, near, low, high):
    first = by_core(near, [(1, 0), (1, 1)])
    second = by_core(jnp.where(at["far"], high, low), [(2, 1), (2, 0)])
    mine = jnp.concatenate([cells(first), cells(second)], axis=0)
    return mine, to_core(mine)


def body(rhs, shift, slots, coarse_inverse):
    where, at = place()
    where, at, rhs = lax.optimization_barrier((where, at, rhs))
    right = jnp.transpose(rhs, (1, 2, 0, 3))
    n = right.shape[0]
    tail = chans, depth = right.shape[2:]
    half, size = n // 2, n // 4

    x0, q0, b1, shift_wide, shift_one, shift_two = call(
        functools.partial(down_fine_kernel, n, grid_of(n)),
        where,
        [right, *frame(at, right, HALO, shift), shift],
        [
            (n, n) + tail,
            (n, n) + tail,
            (half, half) + tail,
            (3 * n, 3 * n, depth),
            (half + 4, half + 4, depth),
            (3 * size, 3 * size, depth),
        ],
        [(3 * half, 2 * n, depth), (n + 6, n + 6) + tail, (n + 4, n + 4) + tail, (n + 2, n + 2) + tail],
        "down_fine",
    )
    x1, q1, b2 = call(
        functools.partial(down_kernel, half, grid_of(half)),
        where,
        [b1, *frame(at, b1, HALO), shift_one],
        [(half, half) + tail, (half, half) + tail, (size, size) + tail],
        [(half + 6, half + 6) + tail, (half + 4, half + 4) + tail, (half + 2, half + 2) + tail],
        "down_middle",
    )

    first_core = at["gy"]
    edge = jnp.where(first_core, shift_two[:, : 2 * size], shift_two[:, size:])
    edge_rows = edge.shape[0] * edge.shape[1]
    spare = -edge_rows % chans
    slot = jnp.broadcast_to(slots.astype(jnp.float32), (chans, depth))
    message = [cells(b2), jnp.pad(edge.reshape(-1, depth), ((0, spare), (0, 0))).reshape(-1, chans, depth), slot[None]]
    other = to_core(jnp.concatenate(message, axis=0))
    other_slot = other[-1]
    slot_rows = [jnp.where(first_core, slot, other_slot)[:8], jnp.where(first_core, other_slot, slot)[:8]]
    edge = other[size * size :].reshape(-1, depth)[:edge_rows].reshape(edge.shape)
    other = other[: size * size].reshape(b2.shape)
    chip = jnp.concatenate([jnp.where(first_core, b2, other), jnp.where(first_core, other, b2)], axis=1)
    mine, others = lines_around(at, chip, chip[:1], chip[1:])
    near, wide = 2 * size * size, (1, 2 * size, chans, depth)
    mine_first, other_first = mine[:near].reshape(chip.shape), others[:near].reshape(chip.shape)
    mine_far, other_far = mine[near:].reshape(wide), others[near:].reshape(wide)
    rows = jnp.concatenate(
        [
            jnp.where(at["far"], other_far, mine_far),
            jnp.where(at["line"], other_first, mine_first),
            chip,
            jnp.where(at["line"], mine_first, other_first),
            jnp.where(at["far"], mine_far, other_far),
        ],
        axis=0,
    )
    blocks = lax.axis_size("gy")
    pairs = []
    for j in range(blocks - 2):
        if (j // 2) % 2 == j % 2:
            pairs += [(j, j + 2), (j + 2, j)]
    mine = lax.ppermute(jnp.where(at["chip"], rows[1:-1, 1:], rows[1:-1, :-1]), "gy", pairs)
    others = to_core(mine)
    ends = [jnp.where(at["chip"], others, mine), jnp.where(at["chip"], mine, others)]
    ends = [jnp.pad(end, ((1, 1), (0, 0), (0, 0), (0, 0))) for end in ends]
    pad = jnp.concatenate([ends[0], rows, ends[1]], axis=1)
    chip_shift = jnp.where(
        first_core,
        jnp.concatenate([shift_two[:, : 2 * size], edge], axis=1),
        jnp.concatenate([edge, shift_two[:, size:]], axis=1),
    )
    x2, q2, b3 = call(
        functools.partial(down_chip_kernel, (size, 2 * size), grid_of(size)),
        where,
        [pad, chip_shift],
        [(size, 2 * size) + tail, (size, 2 * size) + tail, (1, 2) + tail],
        [(size + 4, 2 * size + 4) + tail, (size + 2, 2 * size + 2) + tail],
        "down_chip",
    )
    x2, q2 = [jnp.where(first_core, v[:, :size], v[:, size:]) for v in (x2, q2)]

    lefts = [q0, q1, q2]
    low = jnp.concatenate([cells(q[:2]) for q in lefts], axis=0)
    high = jnp.concatenate([cells(q[-2:]) for q in lefts], axis=0)
    left_ends = swap_ends(at, low, high, "gx", 1)

    line = [list(range(first, blocks, 2)) for first in range(2)]
    shares = lax.all_gather(
        jnp.concatenate([b3[0, 0], b3[0, 1], *slot_rows], axis=0)[None], "gy", axis_index_groups=line, axis=0, tiled=True
    )
    left_ends, shares = lax.optimization_barrier((left_ends, shares))
    before, after = in_order(at, *left_ends, "gx")
    left_rows, done = [], 0
    for q in lefts:
        strip = 2 * q.shape[1]
        shape = (2,) + q.shape[1:]
        ends = [side[done : done + strip].reshape(shape) for side in (before, after)]
        left_rows.append(jnp.concatenate([ends[0], q, ends[1]], axis=0))
        done += strip
    low = jnp.concatenate([cells(q[:, :2]) for q in left_rows], axis=0)
    high = jnp.concatenate([cells(q[:, -2:]) for q in left_rows], axis=0)
    left_sides = swap_ends(at, low, high, "gy", 1)
    offsets = [0, 2 * (n + 4), 2 * (n + 4) + 2 * (half + 4)]

    solved = call(
        solve_kernel, where, [shares, coarse_inverse[0, 0]], [tail], [(chans, blocks * depth)], "solve"
    )[0]
    other = to_core(solved)
    solved = jnp.concatenate([jnp.where(first_core, solved, other), jnp.where(first_core, other, solved)], axis=0)
    back = lax.all_gather(solved[None], "gy", axis_index_groups=line, axis=0, tiled=True)
    fix = call(pick_kernel, where, [shares, back], [(6,) + tail], [], "pick")[0]
    lines = lines_around(at, fix, fix, fix)

    x2 = up(size, where, fix, lines, shift_two, (0, 0), x2, left_rows[2], left_sides, offsets[2])
    x1 = up(half, where, x2, frame(at, x2, 2), shift_one, (0, 0), x1, left_rows[1], left_sides, offsets[1])
    x0 = up(n, where, x1, frame(at, x1, 2), shift_wide, (n - 2, n - 2), x0, left_rows[0], left_sides, offsets[0])
    return jnp.transpose(x0, (2, 0, 1, 3))


def solution(mesh):
    return jax.shard_map(
        body,
        mesh=mesh,
        in_specs=(
            P(None, "gx", "gy", None),
            P("gx", "gy", None),
            P("gx", "gy"),
            P("gx", "gy", None, None),
        ),
        out_specs=P(None, "gx", "gy", None),
        check_vma=False,
    )
```

```python
import functools
import math

import jax
import jax.numpy as jnp
from jax import lax
from jax.experimental import pallas as pl
from jax.experimental.pallas import tpu as pltpu
from jax.sharding import PartitionSpec as P

THETA = 8.0
DELTA = 6.5
ROOTS = tuple(THETA + DELTA * math.cos(math.pi * (2 * k + 1) / 6) for k in range(3))
HALO = 3


def swap(x, axis, dist, odd):
    count = lax.axis_size(axis)
    pairs = []
    for i in range(count - dist):
        if (i // dist) % 2 == odd:
            pairs += [(i, i + dist), (i + dist, i)]
    return lax.ppermute(x, axis, pairs)


def parity(axis, dist):
    return lax.rem(lax.div(lax.axis_index(axis), dist), 2)


def swap_ends(at, low, high, axis, dist):
    even = at[axis]
    first = swap(jnp.where(even, high, low), axis, dist, 0)
    second = swap(jnp.where(even, low, high), axis, dist, 1)
    return first, second


def in_order(at, first, second, axis):
    even = at[axis]
    return jnp.where(even, second, first), jnp.where(even, first, second)


def cells(x):
    return x.reshape((-1,) + x.shape[-2:])


def z_neighbours(v):
    lane = lax.broadcasted_iota(jnp.int32, v.shape, 1)
    below = jnp.where(lane == 0, 0.0, pltpu.roll(v, 1, 1))
    above = jnp.where(lane == v.shape[1] - 1, 0.0, pltpu.roll(v, v.shape[1] - 1, 1))
    return below + above


def inside(at, size):
    return jnp.where((at >= 0) & (at < size), 1.0, 0.0).astype(jnp.float32)


def beside(src, x, y):
    centre = src[x, y]
    total = (src[x - 1, y] + src[x + 1, y]) + (src[x, y - 1] + src[x, y + 1])
    return total + z_neighbours(centre), centre


def factor_cell(src, x, y, shift_row, root, mask):
    total, centre = beside(src, x, y)
    scale = mask * (1.0 / root)
    return (scale * ((root - 6.0) - shift_row)) * centre + scale * total


def each_row(count, row):
    if count <= 4:
        for x in range(count):
            row(x)
        return

    def pair(step, carry):
        row(2 * step)
        row(2 * step + 1)
        return carry

    lax.fori_loop(0, count // 2, pair, 0)


def factor(src, dst, shift, shift_at, size, root, masks):
    def row(x):
        row_mask = masks(x, None)
        for y in range(size[1]):
            shift_row = shift[x + shift_at[0], pl.ds(y + shift_at[1], 1), :]
            mask = row_mask * masks(None, y)
            dst[x, y] = factor_cell(src, x + 1, y + 1, shift_row, root, mask)

    each_row(size[0], row)


def masks_of(first, reach, grid):
    def masks(x, y):
        if x is not None:
            return inside(first[0] + x - reach, grid[0])
        return inside(first[1] + y - reach, grid[1])

    return masks


def put_frame(dst, own, pieces, where, n, width):
    x_even, x_odd, y_even, y_odd = pieces
    high = n + width
    rows = [jnp.where(where[3] == odd, high, 0) for odd in (0, 1)]
    columns = [jnp.where(where[2] == odd, high, 0) for odd in (0, 1)]

    def middle(x):
        for y in range(n):
            dst[x + width, y + width] = own[x, y]

    def outer(x):
        for ref, at in ((x_even, rows[0]), (x_odd, rows[1])):
            for y in range(n):
                dst[at + x, width + y] = ref[x * n + y]

    def beside(x):
        for ref, at in ((y_even, columns[0]), (y_odd, columns[1])):
            for k in range(width):
                dst[x, at + k] = ref[x * width + k]

    each_row(n, middle)
    for x in range(width):
        outer(x)
    each_row(n + 2 * width, beside)


def put_columns(dst, centre, pieces, where, rows, width, reach):
    def row(x):
        for y in range(width):
            dst[x, reach + y] = centre[x, y]
        for ref, base, odd in pieces:
            at = jnp.where(where[2] == odd, reach + width, 0)
            for k in range(reach):
                dst[x, at + k] = ref[base + x * reach + k]

    each_row(rows, row)


def put_shift(wide, one, one_wide, two, own, pieces, where, n):
    x_even, x_odd, y_even, y_odd = pieces
    chans = x_even.shape[1]
    strip, side = HALO * n, HALO * (n + 2 * HALO)

    def line(ref, first, x):
        at = x * n
        return ref[first + at // chans, at % chans : at % chans + n, :]

    for odd, x_ref, y_ref in ((0, x_even, y_even), (1, x_odd, y_odd)):
        row = jnp.where(where[3] == odd, 2 * n, 0)
        column = pl.ds(pl.multiple_of(jnp.where(where[2] == odd, 2 * n, 0), n), n)
        for x in range(n):
            wide[row + x, n : 2 * n, :] = line(x_ref, strip, x)
        for x in range(3 * n):
            wide[x, column, :] = line(y_ref, side, x)
    for x in range(n):
        wide[n + x, n : 2 * n, :] = own[x]

    def halve(src, x, count):
        total = 0.0
        for k in range(4):
            total = total + src[2 * x + k // 2, pl.ds(k % 2, count, 2), :]
        return 0.25 * total

    half = n // 2
    for x in range(3 * half):
        row = halve(wide, x, 3 * half)
        one_wide[x, 0 : 3 * half, :] = row
        if half - 2 <= x < 2 * half + 2:
            one[x - half + 2] = row[half - 2 : 2 * half + 2]
    for x in range(3 * half // 2):
        two[x] = halve(one_wide, x, 3 * half // 2)


def down_body(size, grid, first, pad, shift, shift_at, iterate, leftover, coarser, one, two):
    nx, ny = size
    sx, sy = shift_at
    factor(pad, one, shift, (sx, sy), (nx + 4, ny + 4), ROOTS[0], masks_of(first, 2, grid))
    factor(one, two, shift, (sx + 1, sy + 1), (nx + 2, ny + 2), ROOTS[1], masks_of(first, 1, grid))

    def row(x):
        for y in range(ny):
            shift_row = shift[x + 2 + sx, pl.ds(y + 2 + sy, 1), :]
            leftover[x, y] = factor_cell(two, x + 1, y + 1, shift_row, ROOTS[2], 1.0)
            iterate[x, y] = (
                pad[x + 3, y + 3] * (1.0 / ROOTS[0])
                + one[x + 2, y + 2] * (1.0 / ROOTS[1])
                + two[x + 1, y + 1] * (1.0 / ROOTS[2])
            )

    each_row(nx, row)

    def coarse_row(x):
        for y in range(ny // 2):
            near = leftover[2 * x, 2 * y] + leftover[2 * x, 2 * y + 1]
            far = leftover[2 * x + 1, 2 * y] + leftover[2 * x + 1, 2 * y + 1]
            coarser[x, y] = 0.25 * (near + far)

    each_row(nx // 2, coarse_row)


def down_fine_kernel(n, grid, where, own, *refs):
    pieces, own_shift = refs[:4], refs[4]
    iterate, leftover, coarser, shift, shift_one, shift_two, one_wide, pad, one, two = refs[5:]
    put_frame(pad, own, pieces, where, n, HALO)
    put_shift(shift, shift_one, one_wide, shift_two, own_shift, pieces, where, n)
    first = (where[0] * n, where[1] * n)
    down_body((n, n), grid, first, pad, shift, (n - 2, n - 2), iterate, leftover, coarser, one, two)


def down_kernel(n, grid, where, own, *refs):
    pieces, shift = refs[:4], refs[4]
    iterate, leftover, coarser, pad, one, two = refs[5:]
    put_frame(pad, own, pieces, where, n, HALO)
    first = (where[0] * n, where[1] * n)
    down_body((n, n), grid, first, pad, shift, (0, 0), iterate, leftover, coarser, one, two)


def down_chip_kernel(size, grid, where, pad, shift, iterate, leftover, coarser, one, two):
    first = (where[0] * size[0], (where[1] - where[2]) * size[0])
    down_body(size, grid, first, pad, shift, (0, 0), iterate, leftover, coarser, one, two)


def solve_kernel(where, shares, inverse, solved, ordered):
    count, rows, depth = shares.shape
    chans = solved.shape[0]
    for m in range(count):
        block = jnp.zeros((chans, depth), jnp.float32)
        for j in range(count):
            block = jnp.where(shares[j, chans : chans + 1, :] == float(m), shares[j, 0:chans, :], block)
        ordered[:, m * depth : (m + 1) * depth] = block
    solved[...] = lax.dot_general(
        ordered[...],
        inverse[...],
        (((1,), (1,)), ((), ())),
        precision=lax.Precision.HIGHEST,
        preferred_element_type=jnp.float32,
    )


def pick_kernel(where, shares, back, picked):
    count, chans, depth = back.shape
    for k in range(picked.shape[0]):
        j = where[1] - where[2] + k - 2
        slot = shares[jnp.clip(j, 0, count - 1), pl.ds(chans, 1), :]
        slot = jnp.where((j >= 0) & (j < count), slot, -1.0)
        block = jnp.zeros((chans, depth), jnp.float32)
        for m in range(count):
            block = jnp.where(slot == float(m), back[m], block)
        picked[k] = block


def up_kernel(n, grid, shift_at, offset, pieces_count, where, coarse_own, *refs):
    half = n // 2
    sx, sy = shift_at
    pieces = refs[:pieces_count]
    shift, iterate, leftover_rows, left_even, left_odd, result, coarse, start, one = refs[pieces_count:]
    if pieces_count == 2:
        mine, others = pieces
        core, line, far = where[2], where[4], where[5]
        for k in range(5):
            coarse[2, k] = coarse_own[core + k]
            coarse[3 - 2 * line, k] = mine[core + k]
            coarse[1 + 2 * line, k] = others[core + k]
            coarse[4 * far, k] = mine[6 + core + k]
            coarse[4 - 4 * far, k] = others[6 + core + k]
    else:
        put_frame(coarse, coarse_own, pieces, where, half, 2)
    put_columns(start, leftover_rows, [(left_even, offset, 0), (left_odd, offset, 1)], where, n + 4, n, 2)
    first = (where[0] * n, where[1] * n)
    outer = masks_of(first, 2, grid)

    def first_row(x):
        row_mask = outer(x, None)
        here, before, after = (x + 2) // 2, (x + 1) // 2, (x + 3) // 2
        for y in range(n + 4):
            at, left, right = (y + 2) // 2, (y + 1) // 2, (y + 3) // 2
            centre = coarse[here, at]
            total = (coarse[before, at] + coarse[after, at]) + (coarse[here, left] + coarse[here, right])
            total = total + z_neighbours(centre)
            shift_row = shift[x + sx, pl.ds(y + sy, 1), :]
            mask = row_mask * outer(None, y)
            start[x, y] = mask * ((start[x, y] - (6.0 + shift_row) * centre) + total)

    each_row(n + 4, first_row)
    factor(start, one, shift, (sx + 1, sy + 1), (n + 2, n + 2), ROOTS[0], masks_of(first, 1, grid))

    def row(x):
        for y in range(n):
            shift_row = shift[x + 2 + sx, pl.ds(y + 2 + sy, 1), :]
            two = factor_cell(one, x + 1, y + 1, shift_row, ROOTS[1], 1.0)
            step = (
                start[x + 2, y + 2] * (1.0 / ROOTS[0]) + one[x + 1, y + 1] * (1.0 / ROOTS[1]) + two * (1.0 / ROOTS[2])
            )
            result[x, y] = (iterate[x, y] + coarse[x // 2 + 2, y // 2 + 2]) + step

    each_row(n, row)


VMEM = pl.BlockSpec(memory_space=pltpu.VMEM)
SMEM = pl.BlockSpec(memory_space=pltpu.SMEM)


def call(kernel, where, operands, outs, scratch, name):
    return pl.pallas_call(
        kernel,
        out_shape=[jax.ShapeDtypeStruct(out, jnp.float32) for out in outs],
        in_specs=[SMEM] + [VMEM] * len(operands),
        out_specs=[VMEM] * len(outs),
        scratch_shapes=[pltpu.VMEM(own, jnp.float32) for own in scratch],
        compiler_params=pltpu.CompilerParams(vmem_limit_bytes=12 * 1024 * 1024),
        name=name,
    )(where, *operands)


def place():
    core = parity("gy", 1)
    line, far = parity("gx", 1), parity("gx", 2)
    numbers = [lax.axis_index("gx"), lax.axis_index("gy"), core, line, line ^ core, far ^ core]
    where = jnp.stack(numbers + [jnp.zeros_like(core)] * 2).astype(jnp.int32)
    sides = {
        "gx": line == 0,
        "gy": core == 0,
        "line": line == core,
        "far": far != core,
        "chip": parity("gy", 2) == core,
    }
    return where, sides


def grid_of(n):
    return (lax.axis_size("gx") * n, lax.axis_size("gy") * n)


def up(n, where, coarse_own, pieces, shift, shift_at, iterate, leftover_rows, left, offset):
    tail = iterate.shape[-2:]
    return call(
        functools.partial(up_kernel, n, grid_of(n), shift_at, offset, len(pieces)),
        where,
        [coarse_own, *pieces, shift, iterate, leftover_rows, *left],
        [(n, n) + tail],
        [(n // 2 + 4, n // 2 + 4) + tail, (n + 4, n + 4) + tail, (n + 2, n + 2) + tail],
        "up_%d" % n,
    )[0]


def frame(at, v, width, blocks=None):
    n = v.shape[0]
    tail = v.shape[-2:]

    def message(strip, rows):
        flat = cells(strip)
        if rows is None:
            return flat
        rows = rows.reshape(-1, tail[1])
        rows = jnp.pad(rows, ((0, -rows.shape[0] % tail[0]), (0, 0)))
        return jnp.concatenate([flat, rows.reshape((-1,) + tail)], axis=0)

    def rows_of(piece):
        flat = piece[width * n :].reshape(-1, tail[1])[: blocks.shape[0] * blocks.shape[1]]
        return flat.reshape(blocks.shape)

    x_pieces = swap_ends(at, message(v[:width], blocks), message(v[n - width :], blocks), "gx", 1)
    sides = in_order(at, *x_pieces, "gx")
    strips = [side[: width * n].reshape((width, n) + tail) for side in sides]
    rows = None
    if blocks is not None:
        rows = jnp.concatenate([rows_of(sides[0]), blocks, rows_of(sides[1])], axis=0)
    low = jnp.concatenate([strips[0][:, :width], v[:, :width], strips[1][:, :width]], axis=0)
    high = jnp.concatenate([strips[0][:, n - width :], v[:, n - width :], strips[1][:, n - width :]], axis=0)
    return [*x_pieces, *swap_ends(at, message(low, rows), message(high, rows), "gy", 1)]


def by_core(x, swaps):
    lines, blocks = lax.axis_size("gx"), lax.axis_size("gy")
    pairs = []
    for j in range(blocks):
        dist, odd = swaps[j % 2]
        for i in range(lines - dist):
            if (i // dist) % 2 == odd:
                pairs += [(i * blocks + j, (i + dist) * blocks + j), ((i + dist) * blocks + j, i * blocks + j)]
    return lax.ppermute(x, ("gx", "gy"), pairs)


def to_core(x):
    return swap(x, "gy", 1, 0)


def lines_around(at, near, low, high):
    first = by_core(near, [(1, 0), (1, 1)])
    second = by_core(jnp.where(at["far"], high, low), [(2, 1), (2, 0)])
    mine = jnp.concatenate([cells(first), cells(second)], axis=0)
    return mine, to_core(mine)


def body(rhs, shift, slots, coarse_inverse):
    where, at = place()
    where, at, rhs = lax.optimization_barrier((where, at, rhs))
    right = jnp.transpose(rhs, (1, 2, 0, 3))
    n = right.shape[0]
    tail = chans, depth = right.shape[2:]
    half, size = n // 2, n // 4

    x0, q0, b1, shift_wide, shift_one, shift_two = call(
        functools.partial(down_fine_kernel, n, grid_of(n)),
        where,
        [right, *frame(at, right, HALO, shift), shift],
        [
            (n, n) + tail,
            (n, n) + tail,
            (half, half) + tail,
            (3 * n, 3 * n, depth),
            (half + 4, half + 4, depth),
            (3 * size, 3 * size, depth),
        ],
        [(3 * half, 2 * n, depth), (n + 6, n + 6) + tail, (n + 4, n + 4) + tail, (n + 2, n + 2) + tail],
        "down_fine",
    )
    x1, q1, b2 = call(
        functools.partial(down_kernel, half, grid_of(half)),
        where,
        [b1, *frame(at, b1, HALO), shift_one],
        [(half, half) + tail, (half, half) + tail, (size, size) + tail],
        [(half + 6, half + 6) + tail, (half + 4, half + 4) + tail, (half + 2, half + 2) + tail],
        "down_middle",
    )

    first_core = at["gy"]
    edge = jnp.where(first_core, shift_two[:, : 2 * size], shift_two[:, size:])
    edge_rows = edge.shape[0] * edge.shape[1]
    spare = -edge_rows % chans
    message = jnp.concatenate(
        [cells(b2), jnp.pad(edge.reshape(-1, depth), ((0, spare), (0, 0))).reshape(-1, chans, depth)], axis=0
    )
    other = to_core(message)
    edge = other[size * size :].reshape(-1, depth)[:edge_rows].reshape(edge.shape)
    other = other[: size * size].reshape(b2.shape)
    chip = jnp.concatenate([jnp.where(first_core, b2, other), jnp.where(first_core, other, b2)], axis=1)
    mine, others = lines_around(at, chip, chip[:1], chip[1:])
    near, wide = 2 * size * size, (1, 2 * size, chans, depth)
    mine_first, other_first = mine[:near].reshape(chip.shape), others[:near].reshape(chip.shape)
    mine_far, other_far = mine[near:].reshape(wide), others[near:].reshape(wide)
    rows = jnp.concatenate(
        [
            jnp.where(at["far"], other_far, mine_far),
            jnp.where(at["line"], other_first, mine_first),
            chip,
            jnp.where(at["line"], mine_first, other_first),
            jnp.where(at["far"], mine_far, other_far),
        ],
        axis=0,
    )
    blocks = lax.axis_size("gy")
    pairs = []
    for j in range(blocks - 2):
        if (j // 2) % 2 == j % 2:
            pairs += [(j, j + 2), (j + 2, j)]
    mine = lax.ppermute(jnp.where(at["chip"], rows[1:-1, 1:], rows[1:-1, :-1]), "gy", pairs)
    others = to_core(mine)
    ends = [jnp.where(at["chip"], others, mine), jnp.where(at["chip"], mine, others)]
    ends = [jnp.pad(end, ((1, 1), (0, 0), (0, 0), (0, 0))) for end in ends]
    pad = jnp.concatenate([ends[0], rows, ends[1]], axis=1)
    chip_shift = jnp.where(
        first_core,
        jnp.concatenate([shift_two[:, : 2 * size], edge], axis=1),
        jnp.concatenate([edge, shift_two[:, size:]], axis=1),
    )
    x2, q2, b3 = call(
        functools.partial(down_chip_kernel, (size, 2 * size), grid_of(size)),
        where,
        [pad, chip_shift],
        [(size, 2 * size) + tail, (size, 2 * size) + tail, (1, 2) + tail],
        [(size + 4, 2 * size + 4) + tail, (size + 2, 2 * size + 2) + tail],
        "down_chip",
    )
    x2, q2 = [jnp.where(first_core, v[:, :size], v[:, size:]) for v in (x2, q2)]
    b3 = jnp.where(first_core, b3[0, 0], b3[0, 1])

    lefts = [q0, q1, q2]
    low = jnp.concatenate([cells(q[:2]) for q in lefts], axis=0)
    high = jnp.concatenate([cells(q[-2:]) for q in lefts], axis=0)
    left_ends = swap_ends(at, low, high, "gx", 1)

    slot = jnp.broadcast_to(slots.astype(jnp.float32), (8, depth))
    shares = lax.all_gather(jnp.concatenate([b3, slot], axis=0)[None], "gy", axis=0, tiled=True)
    left_ends, shares = lax.optimization_barrier((left_ends, shares))
    before, after = in_order(at, *left_ends, "gx")
    left_rows, done = [], 0
    for q in lefts:
        strip = 2 * q.shape[1]
        shape = (2,) + q.shape[1:]
        ends = [side[done : done + strip].reshape(shape) for side in (before, after)]
        left_rows.append(jnp.concatenate([ends[0], q, ends[1]], axis=0))
        done += strip
    low = jnp.concatenate([cells(q[:, :2]) for q in left_rows], axis=0)
    high = jnp.concatenate([cells(q[:, -2:]) for q in left_rows], axis=0)
    left_sides = swap_ends(at, low, high, "gy", 1)
    offsets = [0, 2 * (n + 4), 2 * (n + 4) + 2 * (half + 4)]

    solved = call(
        solve_kernel, where, [shares, coarse_inverse[0, 0]], [tail], [(chans, blocks * depth)], "solve"
    )[0]
    back = lax.all_gather(solved[None], "gy", axis=0, tiled=True)
    fix = call(pick_kernel, where, [shares, back], [(6,) + tail], [], "pick")[0]
    lines = lines_around(at, fix, fix, fix)

    x2 = up(size, where, fix, lines, shift_two, (0, 0), x2, left_rows[2], left_sides, offsets[2])
    x1 = up(half, where, x2, frame(at, x2, 2), shift_one, (0, 0), x1, left_rows[1], left_sides, offsets[1])
    x0 = up(n, where, x1, frame(at, x1, 2), shift_wide, (n - 2, n - 2), x0, left_rows[0], left_sides, offsets[0])
    return jnp.transpose(x0, (2, 0, 1, 3))


def solution(mesh):
    return jax.shard_map(
        body,
        mesh=mesh,
        in_specs=(
            P(None, "gx", "gy", None),
            P("gx", "gy", None),
            P("gx", "gy"),
            P("gx", "gy", None, None),
        ),
        out_specs=P(None, "gx", "gy", None),
        check_vma=False,
    )
```

```python
import functools
import math

import jax
import jax.numpy as jnp
from jax import lax
from jax.experimental import pallas as pl
from jax.experimental.pallas import tpu as pltpu
from jax.sharding import PartitionSpec as P

THETA = 8.0
DELTA = 6.5
ROOTS = tuple(THETA + DELTA * math.cos(math.pi * (2 * k + 1) / 6) for k in range(3))
HALO = 3


def swap(x, axis, dist, odd):
    count = lax.axis_size(axis)
    pairs = []
    for i in range(count - dist):
        if (i // dist) % 2 == odd:
            pairs += [(i, i + dist), (i + dist, i)]
    return lax.ppermute(x, axis, pairs)


def parity(axis, dist):
    return lax.rem(lax.div(lax.axis_index(axis), dist), 2)


def swap_ends(at, low, high, axis, dist):
    even = at[axis]
    first = swap(jnp.where(even, high, low), axis, dist, 0)
    second = swap(jnp.where(even, low, high), axis, dist, 1)
    return first, second


def in_order(at, first, second, axis):
    even = at[axis]
    return jnp.where(even, second, first), jnp.where(even, first, second)


def cells(x):
    return x.reshape((-1,) + x.shape[-2:])


def z_neighbours(v):
    lane = lax.broadcasted_iota(jnp.int32, v.shape, 1)
    below = jnp.where(lane == 0, 0.0, pltpu.roll(v, 1, 1))
    above = jnp.where(lane == v.shape[1] - 1, 0.0, pltpu.roll(v, v.shape[1] - 1, 1))
    return below + above


def inside(at, size):
    return jnp.where((at >= 0) & (at < size), 1.0, 0.0).astype(jnp.float32)


def beside(src, x, y):
    centre = src[x, y]
    total = (src[x - 1, y] + src[x + 1, y]) + (src[x, y - 1] + src[x, y + 1])
    return total + z_neighbours(centre), centre


def factor_cell(src, x, y, shift_row, root, mask):
    total, centre = beside(src, x, y)
    scale = mask * (1.0 / root)
    return (scale * ((root - 6.0) - shift_row)) * centre + scale * total


def each_row(count, row):
    if count <= 4:
        for x in range(count):
            row(x)
        return

    def pair(step, carry):
        row(2 * step)
        row(2 * step + 1)
        return carry

    lax.fori_loop(0, count // 2, pair, 0)


def factor(src, dst, shift, shift_at, size, root, masks):
    def row(x):
        row_mask = masks(x, None)
        for y in range(size[1]):
            shift_row = shift[x + shift_at[0], pl.ds(y + shift_at[1], 1), :]
            mask = row_mask * masks(None, y)
            dst[x, y] = factor_cell(src, x + 1, y + 1, shift_row, root, mask)

    each_row(size[0], row)


def masks_of(first, reach, grid):
    def masks(x, y):
        if x is not None:
            return inside(first[0] + x - reach, grid[0])
        return inside(first[1] + y - reach, grid[1])

    return masks


def triangle_cells(n, reach):
    return sum(n + 2 * (reach - d) for d in range(1, reach + 1))


def put_triangles(dst, pieces, where, n, width, reach):
    for odd, (ref, at) in enumerate(pieces):
        for d in range(1, reach + 1):
            column = jnp.where(where[2] == odd, reach + width - 1 + d, reach - d)
            for x in range(d, n + 2 * reach - d):
                dst[x, column] = ref[at]
                at += 1


def put_frame(dst, own, pieces, where, n, reach, own_at=0):
    x_even, x_odd, y_even, y_odd = pieces

    def middle(x):
        for y in range(n):
            dst[x + reach, y + reach] = own[x + own_at, y + own_at]

    each_row(n, middle)
    for odd, ref in enumerate((x_even, x_odd)):
        at = jnp.where(where[3] == odd, n + reach, 0)
        for x in range(reach):
            for y in range(n):
                dst[at + x, reach + y] = ref[x * n + y]
    put_triangles(dst, [(y_even, 0), (y_odd, 0)], where, n, n, reach)


def put_rows(dst, rows, pieces, where, n, width, reach):
    def row(x):
        for y in range(width):
            dst[x, reach + y] = rows[x, y]

    each_row(n + 2 * reach, row)
    put_triangles(dst, pieces, where, n, width, reach)


def put_shift(wide, one, two, own, pieces, where, n):
    x_even, x_odd, y_even, y_odd = pieces
    chans = x_even.shape[1]
    strip, side = HALO * n, triangle_cells(n, HALO)

    def line(ref, first, x):
        at = x * n
        return ref[first + at // chans, at % chans : at % chans + n, :]

    for odd, x_ref, y_ref in ((0, x_even, y_even), (1, x_odd, y_odd)):
        row = jnp.where(where[3] == odd, 2 * n, 0)
        column = pl.ds(pl.multiple_of(jnp.where(where[2] == odd, 2 * n, 0), n), n)
        for x in range(n):
            wide[row + x, n : 2 * n, :] = line(x_ref, strip, x)
        for x in range(3 * n):
            wide[x, column, :] = line(y_ref, side, x)
    for x in range(n):
        wide[n + x, n : 2 * n, :] = own[x]

    def halve(src, x, count):
        total = 0.0
        for k in range(4):
            total = total + src[2 * x + k // 2, pl.ds(k % 2, count, 2), :]
        return 0.25 * total

    half = n // 2
    for x in range(3 * half):
        one[x] = halve(wide, x, 3 * half)
    for x in range(3 * half // 2):
        two[x] = halve(one, x, 3 * half // 2)


def put_coarse_shift(dst, own, pieces, where, n):
    x_even, x_odd, y_even, y_odd = pieces
    strip, side = HALO * n, triangle_cells(n, HALO)
    wide = own.shape[0]
    for x in range(wide):
        dst[x + 2, 2 : wide + 2, :] = own[x]
    for odd, x_ref, y_ref in ((0, x_even, y_even), (1, x_odd, y_odd)):
        row = jnp.where(where[3] == odd, wide + 2, 0)
        for x in range(2):
            dst[row + x, 2 : wide + 2, :] = x_ref[strip, wide * x : wide * (x + 1), :]

        def aside(after, y_ref=y_ref):
            at = wide + 2 if after else 0
            for x in range(wide + 4):
                dst[x, at : at + 2, :] = y_ref[side, 2 * x : 2 * x + 2, :]

        for value in (0, 1):
            pl.when(where[2] == value)(functools.partial(aside, value == odd))


def down_body(size, beyond, grid, first, pad, shift, shift_at, iterate, leftover, coarser, one, two):
    nx, ny = size[0] + 2 * beyond, size[1] + 2 * beyond
    sx, sy = shift_at
    factor(pad, one, shift, (sx, sy), (nx + 4, ny + 4), ROOTS[0], masks_of(first, beyond + 2, grid))
    factor(one, two, shift, (sx + 1, sy + 1), (nx + 2, ny + 2), ROOTS[1], masks_of(first, beyond + 1, grid))
    masks = masks_of(first, beyond, grid)

    def row(x):
        row_mask = masks(x, None) if beyond else 1.0
        for y in range(ny):
            shift_row = shift[x + 2 + sx, pl.ds(y + 2 + sy, 1), :]
            mask = row_mask * masks(None, y) if beyond else 1.0
            leftover[x, y] = factor_cell(two, x + 1, y + 1, shift_row, ROOTS[2], mask)
            iterate[x, y] = (
                pad[x + 3, y + 3] * (1.0 / ROOTS[0])
                + one[x + 2, y + 2] * (1.0 / ROOTS[1])
                + two[x + 1, y + 1] * (1.0 / ROOTS[2])
            )

    each_row(nx, row)

    def coarse_row(x):
        for y in range(size[1] // 2):
            i, j = 2 * x + beyond, 2 * y + beyond
            near = leftover[i, j] + leftover[i, j + 1]
            far = leftover[i + 1, j] + leftover[i + 1, j + 1]
            coarser[x, y] = 0.25 * (near + far)

    each_row(size[0] // 2, coarse_row)


def down_fine_kernel(n, grid, where, own, *refs):
    pieces, own_shift = refs[:4], refs[4]
    iterate, leftover, coarser, shift, shift_one, shift_two, pad, one, two = refs[5:]
    put_frame(pad, own, pieces, where, n, HALO)
    put_shift(shift, shift_one, shift_two, own_shift, pieces, where, n)
    first = (where[0] * n, where[1] * n)
    down_body((n, n), 0, grid, first, pad, shift, (n - 2, n - 2), iterate, leftover, coarser, one, two)


def down_kernel(n, grid, where, own, *refs):
    pieces, shift, shift_near = refs[:4], refs[4], refs[5]
    iterate, leftover, coarser, shift_wide, pad, one, two = refs[6:]
    put_frame(pad, own, pieces, where, n, HALO)
    put_coarse_shift(shift_wide, shift_near, pieces, where, n)
    first = (where[0] * n, where[1] * n)
    down_body((n, n), 0, grid, first, pad, shift, (2, 2), iterate, leftover, coarser, one, two)


def down_chip_kernel(size, grid, where, rows, left, right, shift, iterate, leftover, coarser, pad, one, two):
    def row(x):
        for y in range(size[1]):
            pad[x, y + 4] = rows[x, y]

    each_row(size[0] + 8, row)
    for ref, base in ((left, 0), (right, 4 + size[1])):
        for y in range(4):
            near = y >= 2 if base == 0 else y < 2
            for x in range(8 if near else 4):
                cell = 2 * x + y % 2 + (0 if near else 16)
                pad[x + (1 if near else 3), base + y] = ref[cell]
    first = (where[0] * size[0], (where[1] - where[2]) * size[0])
    down_body(size, 1, grid, first, pad, shift, (1, 1), iterate, leftover, coarser, one, two)


def solve_kernel(where, shares, inverse, solved, ordered):
    count, rows, depth = shares.shape
    chans = solved.shape[0]
    for m in range(count):
        block = jnp.zeros((chans, depth), jnp.float32)
        for j in range(count):
            block = jnp.where(shares[j, chans : chans + 1, :] == float(m), shares[j, 0:chans, :], block)
        ordered[:, m * depth : (m + 1) * depth] = block
    solved[...] = lax.dot_general(
        ordered[...],
        inverse[...],
        (((1,), (1,)), ((), ())),
        precision=lax.Precision.HIGHEST,
        preferred_element_type=jnp.float32,
    )


def pick_kernel(where, shares, back, picked):
    count, chans, depth = back.shape
    for k in range(picked.shape[0]):
        j = where[1] - where[2] + k - 2
        slot = shares[jnp.clip(j, 0, count - 1), pl.ds(chans, 1), :]
        slot = jnp.where((j >= 0) & (j < count), slot, -1.0)
        block = jnp.zeros((chans, depth), jnp.float32)
        for m in range(count):
            block = jnp.where(slot == float(m), back[m], block)
        picked[k] = block


def up_body(n, beyond, grid, where, coarse, reach, shift, shift_at, iterate, result, start, one):
    sx, sy = shift_at
    first = (where[0] * n, where[1] * n)
    wide = n + 2 * beyond
    outer, masks = masks_of(first, beyond + 2, grid), masks_of(first, beyond, grid)
    offset = 2 * reach - beyond - 2

    def first_row(x):
        row_mask = outer(x, None)
        here, before, after = (x + offset) // 2, (x + offset - 1) // 2, (x + offset + 1) // 2
        for y in range(wide + 4):
            at, left, right = (y + offset) // 2, (y + offset - 1) // 2, (y + offset + 1) // 2
            centre = coarse[here, at]
            total = (coarse[before, at] + coarse[after, at]) + (coarse[here, left] + coarse[here, right])
            total = total + z_neighbours(centre)
            shift_row = shift[x + sx, pl.ds(y + sy, 1), :]
            mask = row_mask * outer(None, y)
            start[x, y] = mask * ((start[x, y] - (6.0 + shift_row) * centre) + total)

    each_row(wide + 4, first_row)
    factor(start, one, shift, (sx + 1, sy + 1), (wide + 2, wide + 2), ROOTS[0], masks_of(first, beyond + 1, grid))

    def row(x):
        row_mask = masks(x, None) if beyond else 1.0
        for y in range(wide):
            shift_row = shift[x + 2 + sx, pl.ds(y + 2 + sy, 1), :]
            mask = row_mask * masks(None, y) if beyond else 1.0
            two = factor_cell(one, x + 1, y + 1, shift_row, ROOTS[1], mask)
            step = (
                start[x + 2, y + 2] * (1.0 / ROOTS[0]) + one[x + 1, y + 1] * (1.0 / ROOTS[1]) + two * (1.0 / ROOTS[2])
            )
            below = coarse[(x - beyond + 2 * reach) // 2, (y - beyond + 2 * reach) // 2]
            result[x, y] = (iterate[x, y] + below) + step

    each_row(wide, row)


def up_block_kernel(n, grid, offset, where, fix, mine, others, shift, iterate, rows, even, odd, result, coarse, start, one):
    core, line, far = where[2], where[4], where[5]
    for k in range(5):
        coarse[2, k] = fix[core + k]
        coarse[3 - 2 * line, k] = mine[core + k]
        coarse[1 + 2 * line, k] = others[core + k]
        coarse[4 * far, k] = mine[6 + core + k]
        coarse[4 - 4 * far, k] = others[6 + core + k]
    put_rows(start, rows, [(even, offset), (odd, offset)], where, n, n, 3)
    up_body(n, 1, grid, where, coarse, 2, shift, (1, 1), iterate, result, start, one)


def up_middle_kernel(
    n, grid, offset, iterate_offset, where, coarse_own, x_even, x_odd, y_even, y_odd, shift, iterate_rows, rows, even, odd,
    result, coarse, iterate, start, one,
):
    put_frame(coarse, coarse_own, [x_even, x_odd, y_even, y_odd], where, n // 2, 3, 1)
    put_rows(start, rows, [(even, offset), (odd, offset)], where, n, n, 4)
    put_rows(iterate, iterate_rows, [(even, iterate_offset), (odd, iterate_offset)], where, n, n, 2)
    up_body(n, 2, grid, where, coarse, 3, shift, (0, 0), iterate, result, start, one)


def up_fine_kernel(n, grid, offset, where, coarse, shift, iterate, rows, even, odd, result, start, one):
    put_rows(start, rows, [(even, offset), (odd, offset)], where, n, n, 2)
    up_body(n, 0, grid, where, coarse, 2, shift, (n - 2, n - 2), iterate, result, start, one)


VMEM = pl.BlockSpec(memory_space=pltpu.VMEM)
SMEM = pl.BlockSpec(memory_space=pltpu.SMEM)


def call(kernel, where, operands, outs, scratch, name):
    return pl.pallas_call(
        kernel,
        out_shape=[jax.ShapeDtypeStruct(out, jnp.float32) for out in outs],
        in_specs=[SMEM] + [VMEM] * len(operands),
        out_specs=[VMEM] * len(outs),
        scratch_shapes=[pltpu.VMEM(own, jnp.float32) for own in scratch],
        compiler_params=pltpu.CompilerParams(vmem_limit_bytes=12 * 1024 * 1024),
        name=name,
    )(where, *operands)


def place():
    core = parity("gy", 1)
    line, far = parity("gx", 1), parity("gx", 2)
    numbers = [lax.axis_index("gx"), lax.axis_index("gy"), core, line, line ^ core, far ^ core]
    where = jnp.stack(numbers + [jnp.zeros_like(core)] * 2).astype(jnp.int32)
    sides = {
        "gx": line == 0,
        "gy": core == 0,
        "line": line == core,
        "far": far != core,
        "chip": parity("gy", 2) == core,
    }
    return where, sides


def grid_of(n):
    return (lax.axis_size("gx") * n, lax.axis_size("gy") * n)


def triangle(columns, n, reach):
    parts = []
    for d, column in enumerate(columns, 1):
        over = (column.shape[0] - n) // 2 - (reach - d)
        parts.append(column[over : column.shape[0] - over])
    return jnp.concatenate(parts, axis=0)


def columns_of(rows, reach):
    width = rows.shape[1]
    return [rows[:, d] for d in range(reach)], [rows[:, width - 1 - d] for d in range(reach)]


def with_rows(strip, rows, tail):
    if rows is None:
        return strip
    rows = rows.reshape(-1, tail[1])
    rows = jnp.pad(rows, ((0, -rows.shape[0] % tail[0]), (0, 0)))
    return jnp.concatenate([strip, rows.reshape((-1,) + tail)], axis=0)


def frame(at, v, reach, beyond=0, blocks=None, rims=None):
    n = v.shape[0] - 2 * beyond
    tail = v.shape[-2:]
    own = v[beyond : beyond + n, beyond : beyond + n]
    extra = [blocks, blocks] if rims is None else [rims[-2:], rims[:2]]
    low = v[beyond : beyond + reach, beyond : beyond + n]
    high = v[beyond + n - reach : beyond + n, beyond : beyond + n]
    x_pieces = swap_ends(at, with_rows(cells(low), extra[0], tail), with_rows(cells(high), extra[1], tail), "gx", 1)
    sides = in_order(at, *x_pieces, "gx")
    strips = [side[: reach * n].reshape((reach, n) + tail) for side in sides]
    rows = jnp.concatenate([strips[0], own, strips[1]], axis=0)
    known = min(reach, n)
    low, high = columns_of(rows, known)
    for d in range(known, reach):
        low.append(v[beyond : beyond + n, beyond + d])
        high.append(v[beyond : beyond + n, beyond + n - 1 - d])
    if blocks is not None or rims is not None:
        sent = extra[0].shape

        def rows_of(side):
            return side[reach * n :].reshape(-1, tail[1])[: sent[0] * sent[1]].reshape(sent)

        extra = jnp.concatenate([rows_of(sides[0]), blocks if rims is None else rims, rows_of(sides[1])], axis=0)
        extra = [extra, extra] if rims is None else [extra[:, -2:], extra[:, :2]]
    low, high = triangle(low, n, reach), triangle(high, n, reach)
    y_pieces = swap_ends(at, with_rows(low, extra[0], tail), with_rows(high, extra[1], tail), "gy", 1)
    return [*x_pieces, *y_pieces]


def by_core(x, swaps):
    lines, blocks = lax.axis_size("gx"), lax.axis_size("gy")
    pairs = []
    for j in range(blocks):
        dist, odd = swaps[j % 2]
        for i in range(lines - dist):
            if (i // dist) % 2 == odd:
                pairs += [(i * blocks + j, (i + dist) * blocks + j), ((i + dist) * blocks + j, i * blocks + j)]
    return lax.ppermute(x, ("gx", "gy"), pairs)


def to_core(x):
    return swap(x, "gy", 1, 0)


def lines_around(near):
    first = by_core(near, [(1, 0), (1, 1)])
    second = by_core(near, [(2, 1), (2, 0)])
    mine = jnp.concatenate([cells(first), cells(second)], axis=0)
    return mine, to_core(mine)


def body(rhs, shift, slots, coarse_inverse):
    where, at = place()
    where, at, rhs = lax.optimization_barrier((where, at, rhs))
    right = jnp.transpose(rhs, (1, 2, 0, 3))
    n = right.shape[0]
    tail = chans, depth = right.shape[2:]
    half, size = n // 2, n // 4

    def fields(*shapes):
        return [shape + tail for shape in shapes]

    x0, q0, b1, shift_wide, shift_one, shift_two = call(
        functools.partial(down_fine_kernel, n, grid_of(n)),
        where,
        [right, *frame(at, right, HALO, 0, shift), shift],
        fields((n, n), (n, n), (half, half))
        + [(3 * n, 3 * n, depth), (3 * half, 3 * half, depth), (3 * size, 3 * size, depth)],
        fields((n + 6, n + 6), (n + 4, n + 4), (n + 2, n + 2)),
        "down_fine",
    )
    x1, q1, b2, shift_two = call(
        functools.partial(down_kernel, half, grid_of(half)),
        where,
        [b1, *frame(at, b1, HALO, 0, None, shift_two), shift_one, shift_two],
        fields((half, half), (half, half), (size, size)) + [(3 * size + 4, 3 * size + 4, depth)],
        fields((half + 6, half + 6), (half + 4, half + 4), (half + 2, half + 2)),
        "down_middle",
    )

    first_core = at["gy"]
    edge = jnp.where(first_core, shift_two[:, :2], shift_two[:, -2:])
    other = to_core(with_rows(cells(b2), edge, tail))
    edge = other[size * size :].reshape(-1, depth)[: edge.shape[0] * 2].reshape(edge.shape)
    other = other[: size * size].reshape(b2.shape)
    chip = jnp.concatenate([jnp.where(first_core, b2, other), jnp.where(first_core, other, b2)], axis=1)
    chip_shift = jnp.where(
        first_core, jnp.concatenate([shift_two, edge], axis=1), jnp.concatenate([edge, shift_two], axis=1)
    )
    mine, others = lines_around(chip)
    near = 2 * size * size
    (mine_near, other_near), (mine_far, other_far) = [
        [v[part].reshape(chip.shape) for v in (mine, others)] for part in (slice(0, near), slice(near, 2 * near))
    ]
    rows = jnp.concatenate(
        [
            jnp.where(at["far"], other_far, mine_far),
            jnp.where(at["line"], other_near, mine_near),
            chip,
            jnp.where(at["line"], mine_near, other_near),
            jnp.where(at["far"], mine_far, other_far),
        ],
        axis=0,
    )
    blocks = lax.axis_size("gy")
    pairs = []
    for j in range(blocks - 2):
        if (j // 2) % 2 == j % 2:
            pairs += [(j, j + 2), (j + 2, j)]
    high = jnp.concatenate([cells(rows[1:-1, -2:]), cells(rows[3:-3, :2])], axis=0)
    low = jnp.concatenate([cells(rows[1:-1, :2]), cells(rows[3:-3, -2:])], axis=0)
    mine = lax.ppermute(jnp.where(at["chip"], high, low), "gy", pairs)
    others = to_core(mine)
    x2, q2, b3 = call(
        functools.partial(down_chip_kernel, (size, 2 * size), grid_of(size)),
        where,
        [rows, jnp.where(at["chip"], others, mine), jnp.where(at["chip"], mine, others), chip_shift],
        fields((size + 2, 2 * size + 2), (size + 2, 2 * size + 2), (1, 2)),
        fields((size + 8, 2 * size + 8), (size + 6, 2 * size + 6), (size + 4, 2 * size + 4)),
        "down_chip",
    )
    x2, q2 = [jnp.where(first_core, v[:, : size + 2], v[:, size:]) for v in (x2, q2)]
    b3 = jnp.where(first_core, b3[0, 0], b3[0, 1])

    own = [q0, q1, x1, q2[1:-1, 1:-1]]
    reaches = [2, 4, 2, 3]
    low = jnp.concatenate([cells(q0[:2]), cells(q1), cells(x1[:2]), cells(q2[1:, 1:-1])], axis=0)
    high = jnp.concatenate([cells(q0[-2:]), cells(q1), cells(x1[-2:]), cells(q2[:-1, 1:-1])], axis=0)
    ends = swap_ends(at, low, high, "gx", 1)

    slot = jnp.broadcast_to(slots.astype(jnp.float32), (8, depth))
    shares = lax.all_gather(jnp.concatenate([b3, slot], axis=0)[None], "gy", axis=0, tiled=True)
    ends, shares = lax.optimization_barrier((ends, shares))
    before, after = in_order(at, *ends, "gx")
    around, lows, highs, offsets, done = [], [], [], [0], 0
    for v, reach in zip(own, reaches):
        strip = reach * v.shape[1]
        parts = [side[done : done + strip].reshape((reach,) + v.shape[1:]) for side in (before, after)]
        around.append(jnp.concatenate([parts[0], v, parts[1]], axis=0))
        low, high = columns_of(around[-1], min(reach, v.shape[1]))
        if reach > v.shape[1]:
            low, high = low + [q2[1:-1, -1]], high + [q2[1:-1, 0]]
        lows.append(triangle(low, v.shape[0], reach))
        highs.append(triangle(high, v.shape[0], reach))
        offsets.append(offsets[-1] + lows[-1].shape[0])
        done += strip
    sides = swap_ends(at, jnp.concatenate(lows, axis=0), jnp.concatenate(highs, axis=0), "gy", 1)
    solved = call(
        solve_kernel, where, [shares, coarse_inverse[0, 0]], [tail], [(chans, blocks * depth)], "solve"
    )[0]
    back = lax.all_gather(solved[None], "gy", axis=0, tiled=True)
    fix = call(pick_kernel, where, [shares, back], [(6,) + tail], [], "pick")[0]

    x2 = call(
        functools.partial(up_block_kernel, size, grid_of(size), offsets[3]),
        where,
        [fix, *lines_around(fix), shift_two, x2, around[3], *sides],
        fields((size + 2, size + 2)),
        fields((5, 5), (size + 6, size + 6), (size + 4, size + 4)),
        "up_block",
    )[0]
    x1 = call(
        functools.partial(up_middle_kernel, half, grid_of(half), offsets[1], offsets[2]),
        where,
        [x2, *frame(at, x2, 3, 1), shift_one, around[2], around[1], *sides],
        fields((half + 4, half + 4)),
        fields((size + 6, size + 6), (half + 4, half + 4), (half + 8, half + 8), (half + 6, half + 6)),
        "up_middle",
    )[0]
    x0 = call(
        functools.partial(up_fine_kernel, n, grid_of(n), offsets[0]),
        where,
        [x1, shift_wide, x0, around[0], *sides],
        fields((n, n)),
        fields((n + 4, n + 4), (n + 2, n + 2)),
        "up_fine",
    )[0]
    return jnp.transpose(x0, (2, 0, 1, 3))


def solution(mesh):
    return jax.shard_map(
        body,
        mesh=mesh,
        in_specs=(
            P(None, "gx", "gy", None),
            P("gx", "gy", None),
            P("gx", "gy"),
            P("gx", "gy", None, None),
        ),
        out_specs=P(None, "gx", "gy", None),
        check_vma=False,
    )
```

```python
import functools
import math

import jax
import jax.numpy as jnp
from jax import lax
from jax.experimental import pallas as pl
from jax.experimental.pallas import tpu as pltpu
from jax.sharding import PartitionSpec as P

THETA = 8.0
DELTA = 6.5
ROOTS = tuple(THETA + DELTA * math.cos(math.pi * (2 * k + 1) / 6) for k in range(3))
HALO = 3


def swap(x, axis, dist, odd):
    count = lax.axis_size(axis)
    pairs = []
    for i in range(count - dist):
        if (i // dist) % 2 == odd:
            pairs += [(i, i + dist), (i + dist, i)]
    return lax.ppermute(x, axis, pairs)


def parity(axis, dist):
    return lax.rem(lax.div(lax.axis_index(axis), dist), 2)


def swap_ends(at, low, high, axis, dist):
    even = at[axis]
    first = swap(jnp.where(even, high, low), axis, dist, 0)
    second = swap(jnp.where(even, low, high), axis, dist, 1)
    return first, second


def in_order(at, first, second, axis):
    even = at[axis]
    return jnp.where(even, second, first), jnp.where(even, first, second)


def cells(x):
    return x.reshape((-1,) + x.shape[-2:])


def z_neighbours(v):
    lane = lax.broadcasted_iota(jnp.int32, v.shape, 1)
    below = jnp.where(lane == 0, 0.0, pltpu.roll(v, 1, 1))
    above = jnp.where(lane == v.shape[1] - 1, 0.0, pltpu.roll(v, v.shape[1] - 1, 1))
    return below + above


def inside(at, size):
    return jnp.where((at >= 0) & (at < size), 1.0, 0.0).astype(jnp.float32)


def factor_row(src, x, count, coefficients):
    left, centre = src[x, 0], src[x, 1]
    for y in range(count):
        right = src[x, y + 2]
        shift_row, root, mask = coefficients(y)
        total = (src[x - 1, y + 1] + src[x + 1, y + 1]) + (left + right)
        total = total + z_neighbours(centre)
        scale = mask * (1.0 / root)
        yield (scale * ((root - 6.0) - shift_row)) * centre + scale * total
        left, centre = centre, right


def each_row(count, row):
    if count <= 4:
        for x in range(count):
            row(x)
        return

    def pair(step, carry):
        row(2 * step)
        row(2 * step + 1)
        return carry

    lax.fori_loop(0, count // 2, pair, 0)


def factor(src, dst, shift, shift_at, size, root, masks):
    def row(x):
        row_mask = masks(x, None)

        def coefficients(y):
            return shift[x + shift_at[0], pl.ds(y + shift_at[1], 1), :], root, row_mask * masks(None, y)

        for y, value in enumerate(factor_row(src, x + 1, size[1], coefficients)):
            dst[x, y] = value

    each_row(size[0], row)


def masks_of(first, reach, grid):
    def masks(x, y):
        if x is not None:
            return inside(first[0] + x - reach, grid[0])
        return inside(first[1] + y - reach, grid[1])

    return masks


def triangle_cells(n, reach):
    return sum(n + 2 * (reach - d) for d in range(1, reach + 1))


def put_triangles(dst, pieces, where, n, width, reach):
    for odd, (ref, at) in enumerate(pieces):
        for d in range(1, reach + 1):
            column = jnp.where(where[2] == odd, reach + width - 1 + d, reach - d)
            for x in range(d, n + 2 * reach - d):
                dst[x, column] = ref[at]
                at += 1


def put_frame(dst, own, pieces, where, n, reach, own_at=0):
    x_even, x_odd, y_even, y_odd = pieces

    def middle(x):
        for y in range(n):
            dst[x + reach, y + reach] = own[x + own_at, y + own_at]

    each_row(n, middle)
    for odd, ref in enumerate((x_even, x_odd)):
        at = jnp.where(where[3] == odd, n + reach, 0)
        for x in range(reach):
            for y in range(n):
                dst[at + x, reach + y] = ref[x * n + y]
    put_triangles(dst, [(y_even, 0), (y_odd, 0)], where, n, n, reach)


def put_rows(dst, rows, pieces, where, n, width, reach):
    def row(x):
        for y in range(width):
            dst[x, reach + y] = rows[x, y]

    each_row(n + 2 * reach, row)
    put_triangles(dst, pieces, where, n, width, reach)


def put_shift(wide, one, two, own, pieces, where, n):
    x_even, x_odd, y_even, y_odd = pieces
    chans = x_even.shape[1]
    strip, side = HALO * n, triangle_cells(n, HALO)

    def line(ref, first, x):
        at = x * n
        return ref[first + at // chans, at % chans : at % chans + n, :]

    for odd, x_ref, y_ref in ((0, x_even, y_even), (1, x_odd, y_odd)):
        row = jnp.where(where[3] == odd, 2 * n, 0)
        column = pl.ds(pl.multiple_of(jnp.where(where[2] == odd, 2 * n, 0), n), n)
        for x in range(n):
            wide[row + x, n : 2 * n, :] = line(x_ref, strip, x)
        for x in range(3 * n):
            wide[x, column, :] = line(y_ref, side, x)
    for x in range(n):
        wide[n + x, n : 2 * n, :] = own[x]

    def halve(src, x, count):
        total = 0.0
        for k in range(4):
            total = total + src[2 * x + k // 2, pl.ds(k % 2, count, 2), :]
        return 0.25 * total

    half = n // 2
    for x in range(3 * half):
        one[x] = halve(wide, x, 3 * half)
    for x in range(3 * half // 2):
        two[x] = halve(one, x, 3 * half // 2)


def put_coarse_shift(dst, own, pieces, where, n):
    x_even, x_odd, y_even, y_odd = pieces
    strip, side = HALO * n, triangle_cells(n, HALO)
    wide = own.shape[0]
    for x in range(wide):
        dst[x + 2, 2 : wide + 2, :] = own[x]
    for odd, x_ref, y_ref in ((0, x_even, y_even), (1, x_odd, y_odd)):
        row = jnp.where(where[3] == odd, wide + 2, 0)
        for x in range(2):
            dst[row + x, 2 : wide + 2, :] = x_ref[strip, wide * x : wide * (x + 1), :]

        def aside(after, y_ref=y_ref):
            at = wide + 2 if after else 0
            for x in range(wide + 4):
                dst[x, at : at + 2, :] = y_ref[side, 2 * x : 2 * x + 2, :]

        for value in (0, 1):
            pl.when(where[2] == value)(functools.partial(aside, value == odd))


def down_body(size, beyond, grid, first, pad, shift, shift_at, iterate, leftover, coarser, one, two):
    nx, ny = size[0] + 2 * beyond, size[1] + 2 * beyond
    sx, sy = shift_at
    factor(pad, one, shift, (sx, sy), (nx + 4, ny + 4), ROOTS[0], masks_of(first, beyond + 2, grid))
    factor(one, two, shift, (sx + 1, sy + 1), (nx + 2, ny + 2), ROOTS[1], masks_of(first, beyond + 1, grid))
    masks = masks_of(first, beyond, grid)

    def row(x):
        row_mask = masks(x, None) if beyond else 1.0

        def coefficients(y):
            mask = row_mask * masks(None, y) if beyond else 1.0
            return shift[x + 2 + sx, pl.ds(y + 2 + sy, 1), :], ROOTS[2], mask

        for y, value in enumerate(factor_row(two, x + 1, ny, coefficients)):
            leftover[x, y] = value
            iterate[x, y] = (
                pad[x + 3, y + 3] * (1.0 / ROOTS[0])
                + one[x + 2, y + 2] * (1.0 / ROOTS[1])
                + two[x + 1, y + 1] * (1.0 / ROOTS[2])
            )

    each_row(nx, row)

    def coarse_row(x):
        for y in range(size[1] // 2):
            i, j = 2 * x + beyond, 2 * y + beyond
            near = leftover[i, j] + leftover[i, j + 1]
            far = leftover[i + 1, j] + leftover[i + 1, j + 1]
            coarser[x, y] = 0.25 * (near + far)

    each_row(size[0] // 2, coarse_row)


def down_fine_kernel(n, grid, where, own, *refs):
    pieces, own_shift = refs[:4], refs[4]
    iterate, leftover, coarser, shift, shift_one, shift_two, pad, one, two = refs[5:]
    put_frame(pad, own, pieces, where, n, HALO)
    put_shift(shift, shift_one, shift_two, own_shift, pieces, where, n)
    first = (where[0] * n, where[1] * n)
    down_body((n, n), 0, grid, first, pad, shift, (n - 2, n - 2), iterate, leftover, coarser, one, two)


def down_kernel(n, grid, where, own, *refs):
    pieces, shift, shift_near = refs[:4], refs[4], refs[5]
    iterate, leftover, coarser, shift_wide, pad, one, two = refs[6:]
    put_frame(pad, own, pieces, where, n, HALO)
    put_coarse_shift(shift_wide, shift_near, pieces, where, n)
    first = (where[0] * n, where[1] * n)
    down_body((n, n), 0, grid, first, pad, shift, (2, 2), iterate, leftover, coarser, one, two)


def down_block_kernel(n, grid, where, rows, near, far, shift, iterate, leftover, coarser, pad, one, two):
    core = where[2]

    def row(x):
        for y in range(2 * n):
            pad[x, 2 * n - n * core + y] = rows[x, y]

    each_row(n + 8, row)
    for ref, at, first, side in ((near, 0, 1, core), (far, 0, n + 1, 1 - core)):
        for d in range(first, 5):
            column = jnp.where(side == 1, n + 3 + d, 4 - d)
            for x in range(d, n + 8 - d):
                pad[x, column] = ref[at]
                at += 1
    first = (where[0] * n, where[1] * n)
    down_body((n, n), 1, grid, first, pad, shift, (1, 1), iterate, leftover, coarser, one, two)


def solve_kernel(where, shares, inverse, solved, ordered):
    count, rows, depth = shares.shape
    chans = solved.shape[0]
    for m in range(count):
        block = jnp.zeros((chans, depth), jnp.float32)
        for j in range(count):
            block = jnp.where(shares[j, chans : chans + 1, :] == float(m), shares[j, 0:chans, :], block)
        ordered[:, m * depth : (m + 1) * depth] = block
    solved[...] = lax.dot_general(
        ordered[...],
        inverse[...],
        (((1,), (1,)), ((), ())),
        precision=lax.Precision.HIGHEST,
        preferred_element_type=jnp.float32,
    )


def pick_kernel(where, shares, back, picked):
    count, chans, depth = back.shape
    for k in range(picked.shape[0]):
        j = where[1] - where[2] + k - 2
        slot = shares[jnp.clip(j, 0, count - 1), pl.ds(chans, 1), :]
        slot = jnp.where((j >= 0) & (j < count), slot, -1.0)
        block = jnp.zeros((chans, depth), jnp.float32)
        for m in range(count):
            block = jnp.where(slot == float(m), back[m], block)
        picked[k] = block


def up_body(n, beyond, grid, where, coarse, reach, shift, shift_at, iterate, result, start, one):
    sx, sy = shift_at
    first = (where[0] * n, where[1] * n)
    wide = n + 2 * beyond
    outer, masks = masks_of(first, beyond + 2, grid), masks_of(first, beyond, grid)
    offset = 2 * reach - beyond - 2

    def first_row(x):
        row_mask = outer(x, None)
        here, before, after = (x + offset) // 2, (x + offset - 1) // 2, (x + offset + 1) // 2
        shared = {}
        for y in range(wide + 4):
            at, left, right = (y + offset) // 2, (y + offset - 1) // 2, (y + offset + 1) // 2
            if at not in shared:
                centre = coarse[here, at]
                shared = {at: (centre, (coarse[before, at] + coarse[after, at]) + z_neighbours(centre))}
            centre, total = shared[at]
            other = coarse[here, left if left != at else right]
            total = total + (centre + other)
            shift_row = shift[x + sx, pl.ds(y + sy, 1), :]
            mask = row_mask * outer(None, y)
            start[x, y] = mask * ((start[x, y] - (6.0 + shift_row) * centre) + total)

    each_row(wide + 4, first_row)
    factor(start, one, shift, (sx + 1, sy + 1), (wide + 2, wide + 2), ROOTS[0], masks_of(first, beyond + 1, grid))

    def row(x):
        row_mask = masks(x, None) if beyond else 1.0

        def coefficients(y):
            mask = row_mask * masks(None, y) if beyond else 1.0
            return shift[x + 2 + sx, pl.ds(y + 2 + sy, 1), :], ROOTS[1], mask

        for y, two in enumerate(factor_row(one, x + 1, wide, coefficients)):
            step = (
                start[x + 2, y + 2] * (1.0 / ROOTS[0]) + one[x + 1, y + 1] * (1.0 / ROOTS[1]) + two * (1.0 / ROOTS[2])
            )
            below = coarse[(x - beyond + 2 * reach) // 2, (y - beyond + 2 * reach) // 2]
            result[x, y] = (iterate[x, y] + below) + step

    each_row(wide, row)


def up_block_kernel(n, grid, offset, where, fix, mine, others, shift, iterate, rows, even, odd, result, coarse, start, one):
    core, line, far = where[2], where[4], where[5]
    for k in range(5):
        coarse[2, k] = fix[core + k]
        coarse[3 - 2 * line, k] = mine[core + k]
        coarse[1 + 2 * line, k] = others[core + k]
        coarse[4 * far, k] = mine[6 + core + k]
        coarse[4 - 4 * far, k] = others[6 + core + k]
    put_rows(start, rows, [(even, offset), (odd, offset)], where, n, n, 3)
    up_body(n, 1, grid, where, coarse, 2, shift, (1, 1), iterate, result, start, one)


def up_last_kernel(n, grids, offsets, where, *refs):
    coarse_own, x_even, x_odd, y_even, y_odd, even, odd = refs[:7]
    shift, iterate_rows, rows, fine_shift, fine_iterate, fine_rows = refs[7:13]
    result, coarse, iterate, start, one, middle, fine_start, fine_one = refs[13:]
    put_frame(coarse, coarse_own, [x_even, x_odd, y_even, y_odd], where, n // 2, 3, 1)
    put_rows(start, rows, [(even, offsets[1]), (odd, offsets[1])], where, n, n, 4)
    put_rows(iterate, iterate_rows, [(even, offsets[2]), (odd, offsets[2])], where, n, n, 2)
    put_rows(fine_start, fine_rows, [(even, offsets[0]), (odd, offsets[0])], where, 2 * n, 2 * n, 2)
    up_body(n, 2, grids[0], where, coarse, 3, shift, (0, 0), iterate, middle, start, one)
    fine_at = (2 * n - 2, 2 * n - 2)
    up_body(2 * n, 0, grids[1], where, middle, 2, fine_shift, fine_at, fine_iterate, result, fine_start, fine_one)


VMEM = pl.BlockSpec(memory_space=pltpu.VMEM)
SMEM = pl.BlockSpec(memory_space=pltpu.SMEM)


def call(kernel, where, operands, outs, scratch, name):
    return pl.pallas_call(
        kernel,
        out_shape=[jax.ShapeDtypeStruct(out, jnp.float32) for out in outs],
        in_specs=[SMEM] + [VMEM] * len(operands),
        out_specs=[VMEM] * len(outs),
        scratch_shapes=[pltpu.VMEM(own, jnp.float32) for own in scratch],
        compiler_params=pltpu.CompilerParams(vmem_limit_bytes=12 * 1024 * 1024),
        name=name,
    )(where, *operands)


def place():
    core = parity("gy", 1)
    line, far = parity("gx", 1), parity("gx", 2)
    numbers = [lax.axis_index("gx"), lax.axis_index("gy"), core, line, line ^ core, far ^ core]
    where = jnp.stack(numbers + [jnp.zeros_like(core)] * 2).astype(jnp.int32)
    sides = {
        "gx": line == 0,
        "gy": core == 0,
        "line": line == core,
        "far": far != core,
    }
    return where, sides


def grid_of(n):
    return (lax.axis_size("gx") * n, lax.axis_size("gy") * n)


def triangle(columns, n, reach):
    parts = []
    for d, column in enumerate(columns, 1):
        over = (column.shape[0] - n) // 2 - (reach - d)
        parts.append(column[over : column.shape[0] - over])
    return jnp.concatenate(parts, axis=0)


def columns_of(rows, reach):
    width = rows.shape[1]
    return [rows[:, d] for d in range(reach)], [rows[:, width - 1 - d] for d in range(reach)]


def with_rows(strip, rows, tail):
    if rows is None:
        return strip
    rows = rows.reshape(-1, tail[1])
    rows = jnp.pad(rows, ((0, -rows.shape[0] % tail[0]), (0, 0)))
    return jnp.concatenate([strip, rows.reshape((-1,) + tail)], axis=0)


def frame(at, v, reach, beyond=0, blocks=None, rims=None):
    n = v.shape[0] - 2 * beyond
    tail = v.shape[-2:]
    own = v[beyond : beyond + n, beyond : beyond + n]
    extra = [blocks, blocks] if rims is None else [rims[-2:], rims[:2]]
    low = v[beyond : beyond + reach, beyond : beyond + n]
    high = v[beyond + n - reach : beyond + n, beyond : beyond + n]
    x_pieces = swap_ends(at, with_rows(cells(low), extra[0], tail), with_rows(cells(high), extra[1], tail), "gx", 1)
    sides = in_order(at, *x_pieces, "gx")
    strips = [side[: reach * n].reshape((reach, n) + tail) for side in sides]
    rows = jnp.concatenate([strips[0], own, strips[1]], axis=0)
    known = min(reach, n)
    low, high = columns_of(rows, known)
    for d in range(known, reach):
        low.append(v[beyond : beyond + n, beyond + d])
        high.append(v[beyond : beyond + n, beyond + n - 1 - d])
    if blocks is not None or rims is not None:
        sent = extra[0].shape

        def rows_of(side):
            return side[reach * n :].reshape(-1, tail[1])[: sent[0] * sent[1]].reshape(sent)

        extra = jnp.concatenate([rows_of(sides[0]), blocks if rims is None else rims, rows_of(sides[1])], axis=0)
        extra = [extra, extra] if rims is None else [extra[:, -2:], extra[:, :2]]
    low, high = triangle(low, n, reach), triangle(high, n, reach)
    y_pieces = swap_ends(at, with_rows(low, extra[0], tail), with_rows(high, extra[1], tail), "gy", 1)
    return [*x_pieces, *y_pieces]


def by_core(x, swaps):
    lines, blocks = lax.axis_size("gx"), lax.axis_size("gy")
    pairs = []
    for j in range(blocks):
        dist, odd = swaps[j % 2]
        for i in range(lines - dist):
            if (i // dist) % 2 == odd:
                pairs += [(i * blocks + j, (i + dist) * blocks + j), ((i + dist) * blocks + j, i * blocks + j)]
    return lax.ppermute(x, ("gx", "gy"), pairs)


def to_core(x):
    return swap(x, "gy", 1, 0)


def lines_around(near):
    first = by_core(near, [(1, 0), (1, 1)])
    second = by_core(near, [(2, 1), (2, 0)])
    mine = jnp.concatenate([cells(first), cells(second)], axis=0)
    return mine, to_core(mine)


def body(rhs, shift, slots, coarse_inverse):
    where, at = place()
    where, at, rhs = lax.optimization_barrier((where, at, rhs))
    right = jnp.transpose(rhs, (1, 2, 0, 3))
    n = right.shape[0]
    tail = chans, depth = right.shape[2:]
    half, size = n // 2, n // 4

    def fields(*shapes):
        return [shape + tail for shape in shapes]

    x0, q0, b1, shift_wide, shift_one, shift_two = call(
        functools.partial(down_fine_kernel, n, grid_of(n)),
        where,
        [right, *frame(at, right, HALO, 0, shift), shift],
        fields((n, n), (n, n), (half, half))
        + [(3 * n, 3 * n, depth), (3 * half, 3 * half, depth), (3 * size, 3 * size, depth)],
        fields((n + 6, n + 6), (n + 4, n + 4), (n + 2, n + 2)),
        "down_fine",
    )
    x1, q1, b2, shift_two = call(
        functools.partial(down_kernel, half, grid_of(half)),
        where,
        [b1, *frame(at, b1, HALO, 0, None, shift_two), shift_one, shift_two],
        fields((half, half), (half, half), (size, size)) + [(3 * size + 4, 3 * size + 4, depth)],
        fields((half + 6, half + 6), (half + 4, half + 4), (half + 2, half + 2)),
        "down_middle",
    )

    first_core = at["gy"]
    other = to_core(b2)
    chip = jnp.concatenate([jnp.where(first_core, b2, other), jnp.where(first_core, other, b2)], axis=1)
    mine, others = lines_around(chip)
    near = 2 * size * size
    (mine_near, other_near), (mine_far, other_far) = [
        [v[part].reshape(chip.shape) for v in (mine, others)] for part in (slice(0, near), slice(near, 2 * near))
    ]
    rows = jnp.concatenate(
        [
            jnp.where(at["far"], other_far, mine_far),
            jnp.where(at["line"], other_near, mine_near),
            chip,
            jnp.where(at["line"], mine_near, other_near),
            jnp.where(at["far"], mine_far, other_far),
        ],
        axis=0,
    )
    blocks = lax.axis_size("gy")
    columns = [rows[:, y] for y in range(2 * size)]
    near = jnp.where(first_core, triangle(columns, size, 4), triangle(columns[::-1], size, 4))
    far = [[column[3 + d : -3 - d] for d, column in enumerate(side[:2])] for side in (columns[::-1], columns)]
    far = jnp.where(first_core, *[jnp.concatenate(side, axis=0) for side in far])
    pairs = []
    for j in range(0, blocks - 3, 2):
        pairs += [(j, j + 3), (j + 3, j)]
    x2, q2, b3 = call(
        functools.partial(down_block_kernel, size, grid_of(size)),
        where,
        [rows, swap(near, "gy", 1, 1), lax.ppermute(far, "gy", pairs), shift_two],
        fields((size + 2, size + 2), (size + 2, size + 2), (1, 1)),
        fields((size + 8, size + 8), (size + 6, size + 6), (size + 4, size + 4)),
        "down_block",
    )
    b3 = b3[0, 0]

    own = [q0, q1, x1, q2[1:-1, 1:-1]]
    reaches = [2, 4, 2, 3]
    low = jnp.concatenate([cells(q0[:2]), cells(q1), cells(x1[:2]), cells(q2[1:, 1:-1])], axis=0)
    high = jnp.concatenate([cells(q0[-2:]), cells(q1), cells(x1[-2:]), cells(q2[:-1, 1:-1])], axis=0)
    ends = swap_ends(at, low, high, "gx", 1)

    slot = jnp.broadcast_to(slots.astype(jnp.float32), (8, depth))
    shares = lax.all_gather(jnp.concatenate([b3, slot], axis=0)[None], "gy", axis=0, tiled=True)
    ends, shares = lax.optimization_barrier((ends, shares))
    before, after = in_order(at, *ends, "gx")
    around, lows, highs, offsets, done = [], [], [], [0], 0
    for v, reach in zip(own, reaches):
        strip = reach * v.shape[1]
        parts = [side[done : done + strip].reshape((reach,) + v.shape[1:]) for side in (before, after)]
        around.append(jnp.concatenate([parts[0], v, parts[1]], axis=0))
        low, high = columns_of(around[-1], min(reach, v.shape[1]))
        if reach > v.shape[1]:
            low, high = low + [q2[1:-1, -1]], high + [q2[1:-1, 0]]
        lows.append(triangle(low, v.shape[0], reach))
        highs.append(triangle(high, v.shape[0], reach))
        offsets.append(offsets[-1] + lows[-1].shape[0])
        done += strip
    sides = swap_ends(at, jnp.concatenate(lows, axis=0), jnp.concatenate(highs, axis=0), "gy", 1)
    solved = call(
        solve_kernel, where, [shares, coarse_inverse[0, 0]], [tail], [(chans, blocks * depth)], "solve"
    )[0]
    back = lax.all_gather(solved[None], "gy", axis=0, tiled=True)
    fix = call(pick_kernel, where, [shares, back], [(6,) + tail], [], "pick")[0]

    x2 = call(
        functools.partial(up_block_kernel, size, grid_of(size), offsets[3]),
        where,
        [fix, *lines_around(fix), shift_two, x2, around[3], *sides],
        fields((size + 2, size + 2)),
        fields((5, 5), (size + 6, size + 6), (size + 4, size + 4)),
        "up_block",
    )[0]
    x0 = call(
        functools.partial(up_last_kernel, half, (grid_of(half), grid_of(n)), offsets),
        where,
        [x2, *frame(at, x2, 3, 1), *sides, shift_one, around[2], around[1], shift_wide, x0, around[0]],
        fields((n, n)),
        fields(
            (size + 6, size + 6), (half + 4, half + 4), (half + 8, half + 8), (half + 6, half + 6), (half + 4, half + 4),
            (n + 4, n + 4), (n + 2, n + 2),
        ),
        "up_last",
    )[0]
    return jnp.transpose(x0, (2, 0, 1, 3))


def solution(mesh):
    return jax.shard_map(
        body,
        mesh=mesh,
        in_specs=(
            P(None, "gx", "gy", None),
            P("gx", "gy", None),
            P("gx", "gy"),
            P("gx", "gy", None, None),
        ),
        out_specs=P(None, "gx", "gy", None),
        check_vma=False,
    )
```

```python
import functools
import math

import jax
import jax.numpy as jnp
from jax import lax
from jax.experimental import pallas as pl
from jax.experimental.pallas import tpu as pltpu
from jax.sharding import PartitionSpec as P

THETA = 8.0
DELTA = 6.5
ROOTS = tuple(THETA + DELTA * math.cos(math.pi * (2 * k + 1) / 6) for k in range(3))
HALO = 3


def swap(x, axis, dist, odd):
    count = lax.axis_size(axis)
    pairs = []
    for i in range(count - dist):
        if (i // dist) % 2 == odd:
            pairs += [(i, i + dist), (i + dist, i)]
    return lax.ppermute(x, axis, pairs)


def parity(axis, dist):
    return lax.rem(lax.div(lax.axis_index(axis), dist), 2)


def swap_ends(at, low, high, axis, dist, odd_first=False):
    even = at[axis]
    if odd_first:
        second = swap(jnp.where(even, low, high), axis, dist, 1)
        return swap(jnp.where(even, high, low), axis, dist, 0), second
    first = swap(jnp.where(even, high, low), axis, dist, 0)
    return first, swap(jnp.where(even, low, high), axis, dist, 1)


def in_order(at, first, second, axis):
    even = at[axis]
    return jnp.where(even, second, first), jnp.where(even, first, second)


def cells(x):
    return x.reshape((-1,) + x.shape[-2:])


def z_neighbours(v):
    lane = lax.broadcasted_iota(jnp.int32, v.shape, 1)
    below = jnp.where(lane == 0, 0.0, pltpu.roll(v, 1, 1))
    above = jnp.where(lane == v.shape[1] - 1, 0.0, pltpu.roll(v, v.shape[1] - 1, 1))
    return below + above


def inside(at, size):
    return jnp.where((at >= 0) & (at < size), 1.0, 0.0).astype(jnp.float32)


def factor_row(src, x, count, coefficients):
    left, centre = src[x, 0], src[x, 1]
    for y in range(count):
        right = src[x, y + 2]
        shift_row, root, mask = coefficients(y)
        total = (src[x - 1, y + 1] + src[x + 1, y + 1]) + (left + right)
        total = total + z_neighbours(centre)
        scale = mask * (1.0 / root)
        yield (scale * ((root - 6.0) - shift_row)) * centre + scale * total
        left, centre = centre, right


def each_row(count, row):
    if count <= 4:
        for x in range(count):
            row(x)
        return
    many = 4 if count % 4 == 0 else 2

    def rows(step, carry):
        for k in range(many):
            row(many * step + k)
        return carry

    lax.fori_loop(0, count // many, rows, 0)


def factor(src, dst, shift, shift_at, size, root, masks):
    def row(x):
        row_mask = masks(x, None)

        def coefficients(y):
            return shift[x + shift_at[0], pl.ds(y + shift_at[1], 1), :], root, row_mask * masks(None, y)

        for y, value in enumerate(factor_row(src, x + 1, size[1], coefficients)):
            dst[x, y] = value

    each_row(size[0], row)


def masks_of(first, reach, grid):
    def masks(x, y):
        if x is not None:
            return inside(first[0] + x - reach, grid[0])
        return inside(first[1] + y - reach, grid[1])

    return masks


def triangle_cells(n, reach):
    return sum(n + 2 * (reach - d) for d in range(1, reach + 1))


def put_triangles(dst, pieces, where, n, width, reach):
    for odd, (ref, at) in enumerate(pieces):
        for d in range(1, reach + 1):
            column = jnp.where(where[2] == odd, reach + width - 1 + d, reach - d)
            for x in range(d, n + 2 * reach - d):
                dst[x, column] = ref[at]
                at += 1


def put_frame(dst, own, pieces, where, n, reach, own_at=0):
    x_even, x_odd, y_even, y_odd = pieces

    def middle(x):
        for y in range(n):
            dst[x + reach, y + reach] = own[x + own_at, y + own_at]

    each_row(n, middle)
    for odd, ref in enumerate((x_even, x_odd)):
        at = jnp.where(where[3] == odd, n + reach, 0)
        for x in range(reach):
            for y in range(n):
                dst[at + x, reach + y] = ref[x * n + y]
    put_triangles(dst, [(y_even, 0), (y_odd, 0)], where, n, n, reach)


def put_rows(dst, rows, pieces, where, n, width, reach):
    def row(x):
        for y in range(width):
            dst[x, reach + y] = rows[x, y]

    each_row(n + 2 * reach, row)
    put_triangles(dst, pieces, where, n, width, reach)


def put_shift(wide, one, two, own, pieces, where, n):
    x_even, x_odd, y_even, y_odd = pieces
    chans = x_even.shape[1]
    strip, side = HALO * n, triangle_cells(n, HALO)

    def line(ref, first, x):
        at = x * n
        return ref[first + at // chans, at % chans : at % chans + n, :]

    for odd, x_ref, y_ref in ((0, x_even, y_even), (1, x_odd, y_odd)):
        row = jnp.where(where[3] == odd, 2 * n, 0)
        column = pl.ds(pl.multiple_of(jnp.where(where[2] == odd, 2 * n, 0), n), n)
        for x in range(n):
            wide[row + x, n : 2 * n, :] = line(x_ref, strip, x)
        for x in range(3 * n):
            wide[x, column, :] = line(y_ref, side, x)
    for x in range(n):
        wide[n + x, n : 2 * n, :] = own[x]

    def halve(src, x, count):
        total = 0.0
        for k in range(4):
            total = total + src[2 * x + k // 2, pl.ds(k % 2, count, 2), :]
        return 0.25 * total

    half = n // 2
    for x in range(3 * half):
        one[x] = halve(wide, x, 3 * half)
    for x in range(3 * half // 2):
        two[x] = halve(one, x, 3 * half // 2)


def put_coarse_shift(dst, own, pieces, where, n):
    x_even, x_odd, y_even, y_odd = pieces
    strip, side = HALO * n, triangle_cells(n, HALO)
    wide = own.shape[0]
    for x in range(wide):
        dst[x + 2, 2 : wide + 2, :] = own[x]
    for odd, x_ref, y_ref in ((0, x_even, y_even), (1, x_odd, y_odd)):
        row = jnp.where(where[3] == odd, wide + 2, 0)
        for x in range(2):
            dst[row + x, 2 : wide + 2, :] = x_ref[strip, wide * x : wide * (x + 1), :]

        def aside(after, y_ref=y_ref):
            at = wide + 2 if after else 0
            for x in range(wide + 4):
                dst[x, at : at + 2, :] = y_ref[side, 2 * x : 2 * x + 2, :]

        for value in (0, 1):
            pl.when(where[2] == value)(functools.partial(aside, value == odd))


def down_body(size, beyond, grid, first, pad, shift, shift_at, iterate, leftover, coarser, one, two):
    nx, ny = size[0] + 2 * beyond, size[1] + 2 * beyond
    sx, sy = shift_at
    factor(pad, one, shift, (sx, sy), (nx + 4, ny + 4), ROOTS[0], masks_of(first, beyond + 2, grid))
    factor(one, two, shift, (sx + 1, sy + 1), (nx + 2, ny + 2), ROOTS[1], masks_of(first, beyond + 1, grid))
    masks = masks_of(first, beyond, grid)

    def row(x):
        row_mask = masks(x, None) if beyond else 1.0

        def coefficients(y):
            mask = row_mask * masks(None, y) if beyond else 1.0
            return shift[x + 2 + sx, pl.ds(y + 2 + sy, 1), :], ROOTS[2], mask

        for y, value in enumerate(factor_row(two, x + 1, ny, coefficients)):
            leftover[x, y] = value
            iterate[x, y] = (
                pad[x + 3, y + 3] * (1.0 / ROOTS[0])
                + one[x + 2, y + 2] * (1.0 / ROOTS[1])
                + two[x + 1, y + 1] * (1.0 / ROOTS[2])
            )

    each_row(nx, row)

    def coarse_row(x):
        for y in range(size[1] // 2):
            i, j = 2 * x + beyond, 2 * y + beyond
            near = leftover[i, j] + leftover[i, j + 1]
            far = leftover[i + 1, j] + leftover[i + 1, j + 1]
            coarser[x, y] = 0.25 * (near + far)

    each_row(size[0] // 2, coarse_row)


def down_fine_kernel(n, grid, where, own, *refs):
    pieces, own_shift = refs[:4], refs[4]
    iterate, leftover, coarser, shift, shift_one, shift_two, pad, one, two = refs[5:]
    put_frame(pad, own, pieces, where, n, HALO)
    put_shift(shift, shift_one, shift_two, own_shift, pieces, where, n)
    first = (where[0] * n, where[1] * n)
    down_body((n, n), 0, grid, first, pad, shift, (n - 2, n - 2), iterate, leftover, coarser, one, two)


def down_kernel(n, grid, where, own, *refs):
    pieces, shift, shift_near = refs[:4], refs[4], refs[5]
    iterate, leftover, coarser, shift_wide, pad, one, two = refs[6:]
    put_frame(pad, own, pieces, where, n, HALO)
    put_coarse_shift(shift_wide, shift_near, pieces, where, n)
    first = (where[0] * n, where[1] * n)
    down_body((n, n), 0, grid, first, pad, shift, (2, 2), iterate, leftover, coarser, one, two)


def down_block_kernel(n, grid, where, rows, near, far, shift, iterate, leftover, coarser, pad, one, two):
    core = where[2]

    def row(x):
        for y in range(2 * n):
            pad[x, 2 * n - n * core + y] = rows[x, y]

    each_row(n + 8, row)
    for ref, at, first, side in ((near, 0, 1, core), (far, 0, n + 1, 1 - core)):
        for d in range(first, 5):
            column = jnp.where(side == 1, n + 3 + d, 4 - d)
            for x in range(d, n + 8 - d):
                pad[x, column] = ref[at]
                at += 1
    first = (where[0] * n, where[1] * n)
    down_body((n, n), 1, grid, first, pad, shift, (1, 1), iterate, leftover, coarser, one, two)


def solve_kernel(where, shares, inverse, solved, ordered):
    count, rows, depth = shares.shape
    chans = solved.shape[0]
    for m in range(count):
        block = jnp.zeros((chans, depth), jnp.float32)
        for j in range(count):
            block = jnp.where(shares[j, chans : chans + 1, :] == float(m), shares[j, 0:chans, :], block)
        ordered[:, m * depth : (m + 1) * depth] = block
    solved[...] = lax.dot_general(
        ordered[...],
        inverse[...],
        (((1,), (1,)), ((), ())),
        precision=lax.Precision.HIGHEST,
        preferred_element_type=jnp.float32,
    )


def pick_kernel(where, shares, back, picked):
    count, chans, depth = back.shape
    for k in range(picked.shape[0]):
        j = where[1] - where[2] + k - 2
        slot = shares[jnp.clip(j, 0, count - 1), pl.ds(chans, 1), :]
        slot = jnp.where((j >= 0) & (j < count), slot, -1.0)
        block = jnp.zeros((chans, depth), jnp.float32)
        for m in range(count):
            block = jnp.where(slot == float(m), back[m], block)
        picked[k] = block


def up_body(n, beyond, grid, where, coarse, reach, shift, shift_at, iterate, result, start, one):
    sx, sy = shift_at
    first = (where[0] * n, where[1] * n)
    wide = n + 2 * beyond
    outer, masks = masks_of(first, beyond + 2, grid), masks_of(first, beyond, grid)
    offset = 2 * reach - beyond - 2

    def first_row(x):
        row_mask = outer(x, None)
        here, before, after = (x + offset) // 2, (x + offset - 1) // 2, (x + offset + 1) // 2
        shared = {}
        for y in range(wide + 4):
            at, left, right = (y + offset) // 2, (y + offset - 1) // 2, (y + offset + 1) // 2
            if at not in shared:
                centre = coarse[here, at]
                shared = {at: (centre, (coarse[before, at] + coarse[after, at]) + z_neighbours(centre))}
            centre, total = shared[at]
            other = coarse[here, left if left != at else right]
            total = total + (centre + other)
            shift_row = shift[x + sx, pl.ds(y + sy, 1), :]
            mask = row_mask * outer(None, y)
            start[x, y] = mask * ((start[x, y] - (6.0 + shift_row) * centre) + total)

    each_row(wide + 4, first_row)
    factor(start, one, shift, (sx + 1, sy + 1), (wide + 2, wide + 2), ROOTS[0], masks_of(first, beyond + 1, grid))

    def row(x):
        row_mask = masks(x, None) if beyond else 1.0

        def coefficients(y):
            mask = row_mask * masks(None, y) if beyond else 1.0
            return shift[x + 2 + sx, pl.ds(y + 2 + sy, 1), :], ROOTS[1], mask

        for y, two in enumerate(factor_row(one, x + 1, wide, coefficients)):
            step = (
                start[x + 2, y + 2] * (1.0 / ROOTS[0]) + one[x + 1, y + 1] * (1.0 / ROOTS[1]) + two * (1.0 / ROOTS[2])
            )
            below = coarse[(x - beyond + 2 * reach) // 2, (y - beyond + 2 * reach) // 2]
            result[x, y] = (iterate[x, y] + below) + step

    each_row(wide, row)


def up_block_kernel(n, grid, offset, where, fix, mine, others, shift, iterate, rows, even, odd, result, coarse, start, one):
    core, line, far = where[2], where[4], where[5]
    for k in range(5):
        coarse[2, k] = fix[core + k]
        coarse[3 - 2 * line, k] = mine[core + k]
        coarse[1 + 2 * line, k] = others[core + k]
        coarse[4 * far, k] = mine[6 + core + k]
        coarse[4 - 4 * far, k] = others[6 + core + k]
    put_rows(start, rows, [(even, offset), (odd, offset)], where, n, n, 3)
    up_body(n, 1, grid, where, coarse, 2, shift, (1, 1), iterate, result, start, one)


def up_last_kernel(n, grids, offsets, where, *refs):
    coarse_own, x_even, x_odd, y_even, y_odd, even, odd = refs[:7]
    shift, iterate_rows, rows, fine_shift, fine_iterate, fine_rows = refs[7:13]
    result, coarse, iterate, start, one, middle, fine_start, fine_one = refs[13:]
    put_frame(coarse, coarse_own, [x_even, x_odd, y_even, y_odd], where, n // 2, 3, 1)
    put_rows(start, rows, [(even, offsets[1]), (odd, offsets[1])], where, n, n, 4)
    put_rows(iterate, iterate_rows, [(even, offsets[2]), (odd, offsets[2])], where, n, n, 2)
    put_rows(fine_start, fine_rows, [(even, offsets[0]), (odd, offsets[0])], where, 2 * n, 2 * n, 2)
    up_body(n, 2, grids[0], where, coarse, 3, shift, (0, 0), iterate, middle, start, one)
    fine_at = (2 * n - 2, 2 * n - 2)
    up_body(2 * n, 0, grids[1], where, middle, 2, fine_shift, fine_at, fine_iterate, result, fine_start, fine_one)


VMEM = pl.BlockSpec(memory_space=pltpu.VMEM)


def call(kernel, operands, outs, scratch, name):
    def run(*refs):
        kernel(spot(), *refs)

    return pl.pallas_call(
        run,
        out_shape=[jax.ShapeDtypeStruct(out, jnp.float32) for out in outs],
        in_specs=[VMEM] * len(operands),
        out_specs=[VMEM] * len(outs),
        scratch_shapes=[pltpu.VMEM(own, jnp.float32) for own in scratch],
        compiler_params=pltpu.CompilerParams(vmem_limit_bytes=12 * 1024 * 1024),
        name=name,
    )(*operands)


def place():
    core, line, far = parity("gy", 1), parity("gx", 1), parity("gx", 2)
    return {"gx": line == 0, "gy": core == 0, "line": line == core, "far": far != core}


def spot():
    core, line, far = parity("gy", 1), parity("gx", 1), parity("gx", 2)
    numbers = [lax.axis_index("gx"), lax.axis_index("gy"), core, line]
    return numbers + [lax.rem(line + core, 2), lax.rem(far + core, 2)]


def grid_of(n):
    return (lax.axis_size("gx") * n, lax.axis_size("gy") * n)


def triangle(columns, n, reach):
    parts = []
    for d, column in enumerate(columns, 1):
        over = (column.shape[0] - n) // 2 - (reach - d)
        parts.append(column[over : column.shape[0] - over])
    return jnp.concatenate(parts, axis=0)


def columns_of(rows, reach):
    width = rows.shape[1]
    return [rows[:, d] for d in range(reach)], [rows[:, width - 1 - d] for d in range(reach)]


def with_rows(strip, rows, tail):
    if rows is None:
        return strip
    rows = rows.reshape(-1, tail[1])
    rows = jnp.pad(rows, ((0, -rows.shape[0] % tail[0]), (0, 0)))
    return jnp.concatenate([strip, rows.reshape((-1,) + tail)], axis=0)


def frame(at, v, reach, beyond=0, blocks=None, rims=None, odd_first=False):
    n = v.shape[0] - 2 * beyond
    tail = v.shape[-2:]
    own = v[beyond : beyond + n, beyond : beyond + n]
    extra = [blocks, blocks] if rims is None else [rims[-2:], rims[:2]]
    low = v[beyond : beyond + reach, beyond : beyond + n]
    high = v[beyond + n - reach : beyond + n, beyond : beyond + n]
    low, high = with_rows(cells(low), extra[0], tail), with_rows(cells(high), extra[1], tail)
    x_pieces = swap_ends(at, low, high, "gx", 1, odd_first)
    sides = in_order(at, *x_pieces, "gx")
    strips = [side[: reach * n].reshape((reach, n) + tail) for side in sides]
    rows = jnp.concatenate([strips[0], own, strips[1]], axis=0)
    known = min(reach, n)
    low, high = columns_of(rows, known)
    for d in range(known, reach):
        low.append(v[beyond : beyond + n, beyond + d])
        high.append(v[beyond : beyond + n, beyond + n - 1 - d])
    if blocks is not None or rims is not None:
        sent = extra[0].shape

        def rows_of(side):
            return side[reach * n :].reshape(-1, tail[1])[: sent[0] * sent[1]].reshape(sent)

        extra = jnp.concatenate([rows_of(sides[0]), blocks if rims is None else rims, rows_of(sides[1])], axis=0)
        extra = [extra, extra] if rims is None else [extra[:, -2:], extra[:, :2]]
    low, high = triangle(low, n, reach), triangle(high, n, reach)
    y_pieces = swap_ends(at, with_rows(low, extra[0], tail), with_rows(high, extra[1], tail), "gy", 1)
    return [*x_pieces, *y_pieces]


def by_core(x, swaps):
    lines, blocks = lax.axis_size("gx"), lax.axis_size("gy")
    pairs = []
    for j in range(blocks):
        dist, odd = swaps[j % 2]
        for i in range(lines - dist):
            if (i // dist) % 2 == odd:
                pairs += [(i * blocks + j, (i + dist) * blocks + j), ((i + dist) * blocks + j, i * blocks + j)]
    return lax.ppermute(x, ("gx", "gy"), pairs)


def to_core(x):
    return swap(x, "gy", 1, 0)


def lines_around(near):
    first = by_core(near, [(1, 0), (1, 1)])
    second = by_core(near, [(2, 1), (2, 0)])
    mine = jnp.concatenate([cells(first), cells(second)], axis=0)
    return mine, to_core(mine)


def body(rhs, shift, slots, coarse_inverse):
    at, rhs = lax.optimization_barrier((place(), rhs))
    right = jnp.transpose(rhs, (1, 2, 0, 3))
    n = right.shape[0]
    tail = chans, depth = right.shape[2:]
    half, size = n // 2, n // 4

    def fields(*shapes):
        return [shape + tail for shape in shapes]

    x0, q0, b1, shift_wide, shift_one, shift_two = call(
        functools.partial(down_fine_kernel, n, grid_of(n)),
        [right, *frame(at, right, HALO, 0, shift), shift],
        fields((n, n), (n, n), (half, half))
        + [(3 * n, 3 * n, depth), (3 * half, 3 * half, depth), (3 * size, 3 * size, depth)],
        fields((n + 6, n + 6), (n + 4, n + 4), (n + 2, n + 2)),
        "down_fine",
    )
    x1, q1, b2, shift_two = call(
        functools.partial(down_kernel, half, grid_of(half)),
        [b1, *frame(at, b1, HALO, 0, None, shift_two), shift_one, shift_two],
        fields((half, half), (half, half), (size, size)) + [(3 * size + 4, 3 * size + 4, depth)],
        fields((half + 6, half + 6), (half + 4, half + 4), (half + 2, half + 2)),
        "down_middle",
    )

    first_core = at["gy"]
    other = to_core(b2)
    chip = jnp.concatenate([jnp.where(first_core, b2, other), jnp.where(first_core, other, b2)], axis=1)
    mine, others = lines_around(chip)
    near = 2 * size * size
    (mine_near, other_near), (mine_far, other_far) = [
        [v[part].reshape(chip.shape) for v in (mine, others)] for part in (slice(0, near), slice(near, 2 * near))
    ]
    rows = jnp.concatenate(
        [
            jnp.where(at["far"], other_far, mine_far),
            jnp.where(at["line"], other_near, mine_near),
            chip,
            jnp.where(at["line"], mine_near, other_near),
            jnp.where(at["far"], mine_far, other_far),
        ],
        axis=0,
    )
    blocks = lax.axis_size("gy")
    columns = [rows[:, y] for y in range(2 * size)]
    near = jnp.where(first_core, triangle(columns, size, 4), triangle(columns[::-1], size, 4))
    far = [[column[3 + d : -3 - d] for d, column in enumerate(side[:2])] for side in (columns[::-1], columns)]
    far = jnp.where(first_core, *[jnp.concatenate(side, axis=0) for side in far])
    pairs = []
    for j in range(0, blocks - 3, 2):
        pairs += [(j, j + 3), (j + 3, j)]
    x2, q2, b3 = call(
        functools.partial(down_block_kernel, size, grid_of(size)),
        [rows, swap(near, "gy", 1, 1), lax.ppermute(far, "gy", pairs), shift_two],
        fields((size + 2, size + 2), (size + 2, size + 2), (1, 1)),
        fields((size + 8, size + 8), (size + 6, size + 6), (size + 4, size + 4)),
        "down_block",
    )
    b3 = b3[0, 0]

    own = [q0, q1, x1, q2[1:-1, 1:-1]]
    reaches = [2, 4, 2, 3]
    low = jnp.concatenate([cells(q0[:2]), cells(q1), cells(x1[:2]), cells(q2[1:, 1:-1])], axis=0)
    high = jnp.concatenate([cells(q0[-2:]), cells(q1), cells(x1[-2:]), cells(q2[:-1, 1:-1])], axis=0)
    ends = swap_ends(at, low, high, "gx", 1)

    slot = jnp.broadcast_to(slots.astype(jnp.float32), (8, depth))
    shares = lax.all_gather(jnp.concatenate([b3, slot], axis=0)[None], "gy", axis=0, tiled=True)
    ends, shares = lax.optimization_barrier((ends, shares))
    before, after = in_order(at, *ends, "gx")
    around, lows, highs, offsets, done = [], [], [], [0], 0
    for v, reach in zip(own, reaches):
        strip = reach * v.shape[1]
        parts = [side[done : done + strip].reshape((reach,) + v.shape[1:]) for side in (before, after)]
        around.append(jnp.concatenate([parts[0], v, parts[1]], axis=0))
        low, high = columns_of(around[-1], min(reach, v.shape[1]))
        if reach > v.shape[1]:
            low, high = low + [q2[1:-1, -1]], high + [q2[1:-1, 0]]
        lows.append(triangle(low, v.shape[0], reach))
        highs.append(triangle(high, v.shape[0], reach))
        offsets.append(offsets[-1] + lows[-1].shape[0])
        done += strip
    sides = swap_ends(at, jnp.concatenate(lows, axis=0), jnp.concatenate(highs, axis=0), "gy", 1)
    solved = call(
        solve_kernel, [shares, coarse_inverse[0, 0]], [tail], [(chans, blocks * depth)], "solve"
    )[0]
    back = lax.all_gather(solved[None], "gy", axis=0, tiled=True)
    fix = call(pick_kernel, [shares, back], [(6,) + tail], [], "pick")[0]

    x2 = call(
        functools.partial(up_block_kernel, size, grid_of(size), offsets[3]),
        [fix, *lines_around(fix), shift_two, x2, around[3], *sides],
        fields((size + 2, size + 2)),
        fields((5, 5), (size + 6, size + 6), (size + 4, size + 4)),
        "up_block",
    )[0]
    x0 = call(
        functools.partial(up_last_kernel, half, (grid_of(half), grid_of(n)), offsets),
        [x2, *frame(at, x2, 3, 1, odd_first=True), *sides, shift_one, around[2], around[1], shift_wide, x0, around[0]],
        fields((n, n)),
        fields(
            (size + 6, size + 6), (half + 4, half + 4), (half + 8, half + 8), (half + 6, half + 6), (half + 4, half + 4),
            (n + 4, n + 4), (n + 2, n + 2),
        ),
        "up_last",
    )[0]
    return jnp.transpose(x0, (2, 0, 1, 3))


def solution(mesh):
    return jax.shard_map(
        body,
        mesh=mesh,
        in_specs=(
            P(None, "gx", "gy", None),
            P("gx", "gy", None),
            P("gx", "gy"),
            P("gx", "gy", None, None),
        ),
        out_specs=P(None, "gx", "gy", None),
        check_vma=False,
    )
```

```python
import functools
import math

import jax
import jax.numpy as jnp
from jax import lax
from jax.experimental import pallas as pl
from jax.experimental.pallas import tpu as pltpu
from jax.sharding import PartitionSpec as P

THETA = 8.0
DELTA = 6.5
ROOTS = tuple(THETA + DELTA * math.cos(math.pi * (2 * k + 1) / 6) for k in range(3))
HALO = 3


def swap(x, axis, dist, odd):
    count = lax.axis_size(axis)
    pairs = []
    for i in range(count - dist):
        if (i // dist) % 2 == odd:
            pairs += [(i, i + dist), (i + dist, i)]
    return lax.ppermute(x, axis, pairs)


def parity(axis, dist):
    return lax.rem(lax.div(lax.axis_index(axis), dist), 2)


def swap_ends(at, low, high, axis, dist):
    even = at[axis]
    first = swap(jnp.where(even, high, low), axis, dist, 0)
    return first, swap(jnp.where(even, low, high), axis, dist, 1)


def in_order(at, first, second, axis):
    even = at[axis]
    return jnp.where(even, second, first), jnp.where(even, first, second)


def cells(x):
    return x.reshape((-1,) + x.shape[-2:])


def z_neighbours(v):
    lane = lax.broadcasted_iota(jnp.int32, v.shape, 1)
    below = jnp.where(lane == 0, 0.0, pltpu.roll(v, 1, 1))
    above = jnp.where(lane == v.shape[1] - 1, 0.0, pltpu.roll(v, v.shape[1] - 1, 1))
    return below + above


def inside(at, size):
    return jnp.where((at >= 0) & (at < size), 1.0, 0.0).astype(jnp.float32)


def factor_row(src, x, count, coefficients):
    left, centre = src[x, 0], src[x, 1]
    for y in range(count):
        right = src[x, y + 2]
        shift_row, root, mask = coefficients(y)
        total = (src[x - 1, y + 1] + src[x + 1, y + 1]) + (left + right)
        total = total + z_neighbours(centre)
        scale = mask * (1.0 / root)
        yield (scale * ((root - 6.0) - shift_row)) * centre + scale * total
        left, centre = centre, right


def each_row(count, row):
    if count <= 6:
        for x in range(count):
            row(x)
        return
    many = max(k for k in range(1, 7) if count % k == 0)

    def rows(step, carry):
        for k in range(many):
            row(many * step + k)
        return carry

    lax.fori_loop(0, count // many, rows, 0)


def factor(src, dst, shift, shift_at, size, root, masks):
    def row(x):
        row_mask = masks(x, None)

        def coefficients(y):
            return shift[x + shift_at[0], pl.ds(y + shift_at[1], 1), :], root, row_mask * masks(None, y)

        for y, value in enumerate(factor_row(src, x + 1, size[1], coefficients)):
            dst[x, y] = value

    each_row(size[0], row)


def masks_of(first, reach, grid):
    def masks(x, y):
        if x is not None:
            return inside(first[0] + x - reach, grid[0])
        return inside(first[1] + y - reach, grid[1])

    return masks


def triangle_cells(n, reach):
    return sum(n + 2 * (reach - d) for d in range(1, reach + 1))


def put_triangles(dst, pieces, where, n, width, reach):
    for odd, (ref, at) in enumerate(pieces):
        for d in range(1, reach + 1):
            column = jnp.where(where[2] == odd, reach + width - 1 + d, reach - d)
            for x in range(d, n + 2 * reach - d):
                dst[x, column] = ref[at]
                at += 1


def put_frame(dst, own, pieces, where, n, reach, own_at=0):
    x_even, x_odd, y_even, y_odd = pieces

    def middle(x):
        for y in range(n):
            dst[x + reach, y + reach] = own[x + own_at, y + own_at]

    each_row(n, middle)
    for odd, ref in enumerate((x_even, x_odd)):
        at = jnp.where(where[3] == odd, n + reach, 0)
        for x in range(reach):
            for y in range(n):
                dst[at + x, reach + y] = ref[x * n + y]
    put_triangles(dst, [(y_even, 0), (y_odd, 0)], where, n, n, reach)


def put_rows(dst, rows, pieces, where, n, width, reach):
    def row(x):
        for y in range(width):
            dst[x, reach + y] = rows[x, y]

    each_row(n + 2 * reach, row)
    put_triangles(dst, pieces, where, n, width, reach)


def put_shift(wide, one, two, own, pieces, where, n):
    x_even, x_odd, y_even, y_odd = pieces
    chans = x_even.shape[1]
    strip, side = HALO * n, triangle_cells(n, HALO)

    def line(ref, first, x):
        at = x * n
        return ref[first + at // chans, at % chans : at % chans + n, :]

    for odd, x_ref, y_ref in ((0, x_even, y_even), (1, x_odd, y_odd)):
        row = jnp.where(where[3] == odd, 2 * n, 0)
        column = pl.ds(pl.multiple_of(jnp.where(where[2] == odd, 2 * n, 0), n), n)
        for x in range(n):
            wide[row + x, n : 2 * n, :] = line(x_ref, strip, x)
        for x in range(3 * n):
            wide[x, column, :] = line(y_ref, side, x)
    for x in range(n):
        wide[n + x, n : 2 * n, :] = own[x]

    def halve(src, x, count):
        total = 0.0
        for k in range(4):
            total = total + src[2 * x + k // 2, pl.ds(k % 2, count, 2), :]
        return 0.25 * total

    half = n // 2
    for x in range(3 * half):
        one[x] = halve(wide, x, 3 * half)
    for x in range(3 * half // 2):
        two[x] = halve(one, x, 3 * half // 2)


def put_coarse_shift(dst, own, pieces, where, n):
    x_even, x_odd, y_even, y_odd = pieces
    strip, side = HALO * n, triangle_cells(n, HALO)
    wide = own.shape[0]
    for x in range(wide):
        dst[x + 2, 2 : wide + 2, :] = own[x]
    for odd, x_ref, y_ref in ((0, x_even, y_even), (1, x_odd, y_odd)):
        row = jnp.where(where[3] == odd, wide + 2, 0)
        for x in range(2):
            dst[row + x, 2 : wide + 2, :] = x_ref[strip, wide * x : wide * (x + 1), :]

        def aside(after, y_ref=y_ref):
            at = wide + 2 if after else 0
            for x in range(wide + 4):
                dst[x, at : at + 2, :] = y_ref[side, 2 * x : 2 * x + 2, :]

        for value in (0, 1):
            pl.when(where[2] == value)(functools.partial(aside, value == odd))


def down_body(size, beyond, grid, first, pad, shift, shift_at, iterate, leftover, coarser, one, two):
    nx, ny = size[0] + 2 * beyond, size[1] + 2 * beyond
    sx, sy = shift_at
    factor(pad, one, shift, (sx, sy), (nx + 4, ny + 4), ROOTS[0], masks_of(first, beyond + 2, grid))
    factor(one, two, shift, (sx + 1, sy + 1), (nx + 2, ny + 2), ROOTS[1], masks_of(first, beyond + 1, grid))
    masks = masks_of(first, beyond, grid)

    def row(x):
        row_mask = masks(x, None) if beyond else 1.0

        def coefficients(y):
            mask = row_mask * masks(None, y) if beyond else 1.0
            return shift[x + 2 + sx, pl.ds(y + 2 + sy, 1), :], ROOTS[2], mask

        for y, value in enumerate(factor_row(two, x + 1, ny, coefficients)):
            leftover[x, y] = value
            iterate[x, y] = (
                pad[x + 3, y + 3] * (1.0 / ROOTS[0])
                + one[x + 2, y + 2] * (1.0 / ROOTS[1])
                + two[x + 1, y + 1] * (1.0 / ROOTS[2])
            )

    each_row(nx, row)

    def coarse_row(x):
        for y in range(size[1] // 2):
            i, j = 2 * x + beyond, 2 * y + beyond
            near = leftover[i, j] + leftover[i, j + 1]
            far = leftover[i + 1, j] + leftover[i + 1, j + 1]
            coarser[x, y] = 0.25 * (near + far)

    each_row(size[0] // 2, coarse_row)


def down_fine_kernel(n, grid, where, own, *refs):
    pieces, own_shift = refs[:4], refs[4]
    iterate, leftover, coarser, shift, shift_one, shift_two, pad, one, two = refs[5:]
    put_frame(pad, own, pieces, where, n, HALO)
    put_shift(shift, shift_one, shift_two, own_shift, pieces, where, n)
    first = (where[0] * n, where[1] * n)
    down_body((n, n), 0, grid, first, pad, shift, (n - 2, n - 2), iterate, leftover, coarser, one, two)


def down_kernel(n, grid, where, own, *refs):
    pieces, shift, shift_near = refs[:4], refs[4], refs[5]
    iterate, leftover, coarser, shift_wide, pad, one, two = refs[6:]
    put_frame(pad, own, pieces, where, n, HALO)
    put_coarse_shift(shift_wide, shift_near, pieces, where, n)
    first = (where[0] * n, where[1] * n)
    down_body((n, n), 0, grid, first, pad, shift, (2, 2), iterate, leftover, coarser, one, two)


def down_block_kernel(n, grid, where, rows, near, far, shift, iterate, leftover, coarser, pad, one, two):
    core = where[2]

    def row(x):
        for y in range(2 * n):
            pad[x, 2 * n - n * core + y] = rows[x, y]

    each_row(n + 8, row)
    for ref, at, first, side in ((near, 0, 1, core), (far, 0, n + 1, 1 - core)):
        for d in range(first, 5):
            column = jnp.where(side == 1, n + 3 + d, 4 - d)
            for x in range(d, n + 8 - d):
                pad[x, column] = ref[at]
                at += 1
    first = (where[0] * n, where[1] * n)
    down_body((n, n), 1, grid, first, pad, shift, (1, 1), iterate, leftover, coarser, one, two)


def solve_kernel(where, shares, inverse, solved, ordered):
    count, rows, depth = shares.shape
    chans = solved.shape[0]
    for m in range(count):
        block = jnp.zeros((chans, depth), jnp.float32)
        for j in range(count):
            block = jnp.where(shares[j, chans : chans + 1, :] == float(m), shares[j, 0:chans, :], block)
        ordered[:, m * depth : (m + 1) * depth] = block
    solved[...] = lax.dot_general(
        ordered[...],
        inverse[...],
        (((1,), (1,)), ((), ())),
        precision=lax.Precision.HIGHEST,
        preferred_element_type=jnp.float32,
    )


def pick_kernel(where, shares, back, picked):
    count, chans, depth = back.shape
    for k in range(picked.shape[0]):
        j = where[1] - where[2] + k - 2
        slot = shares[jnp.clip(j, 0, count - 1), pl.ds(chans, 1), :]
        slot = jnp.where((j >= 0) & (j < count), slot, -1.0)
        block = jnp.zeros((chans, depth), jnp.float32)
        for m in range(count):
            block = jnp.where(slot == float(m), back[m], block)
        picked[k] = block


def up_body(n, beyond, grid, where, coarse, reach, shift, shift_at, iterate, result, start, one):
    sx, sy = shift_at
    first = (where[0] * n, where[1] * n)
    wide = n + 2 * beyond
    outer, masks = masks_of(first, beyond + 2, grid), masks_of(first, beyond, grid)
    offset = 2 * reach - beyond - 2

    def first_row(x):
        row_mask = outer(x, None)
        here, before, after = (x + offset) // 2, (x + offset - 1) // 2, (x + offset + 1) // 2
        shared = {}
        for y in range(wide + 4):
            at, left, right = (y + offset) // 2, (y + offset - 1) // 2, (y + offset + 1) // 2
            if at not in shared:
                centre = coarse[here, at]
                shared = {at: (centre, (coarse[before, at] + coarse[after, at]) + z_neighbours(centre))}
            centre, total = shared[at]
            other = coarse[here, left if left != at else right]
            total = total + (centre + other)
            shift_row = shift[x + sx, pl.ds(y + sy, 1), :]
            mask = row_mask * outer(None, y)
            start[x, y] = mask * ((start[x, y] - (6.0 + shift_row) * centre) + total)

    each_row(wide + 4, first_row)
    factor(start, one, shift, (sx + 1, sy + 1), (wide + 2, wide + 2), ROOTS[0], masks_of(first, beyond + 1, grid))

    def row(x):
        row_mask = masks(x, None) if beyond else 1.0

        def coefficients(y):
            mask = row_mask * masks(None, y) if beyond else 1.0
            return shift[x + 2 + sx, pl.ds(y + 2 + sy, 1), :], ROOTS[1], mask

        for y, two in enumerate(factor_row(one, x + 1, wide, coefficients)):
            step = (
                start[x + 2, y + 2] * (1.0 / ROOTS[0]) + one[x + 1, y + 1] * (1.0 / ROOTS[1]) + two * (1.0 / ROOTS[2])
            )
            below = coarse[(x - beyond + 2 * reach) // 2, (y - beyond + 2 * reach) // 2]
            result[x, y] = (iterate[x, y] + below) + step

    each_row(wide, row)


def up_block_kernel(n, grid, offset, where, fix, mine, others, shift, iterate, rows, even, odd, result, coarse, start, one):
    core, line, far = where[2], where[4], where[5]
    for k in range(5):
        coarse[2, k] = fix[core + k]
        coarse[3 - 2 * line, k] = mine[core + k]
        coarse[1 + 2 * line, k] = others[core + k]
        coarse[4 * far, k] = mine[6 + core + k]
        coarse[4 - 4 * far, k] = others[6 + core + k]
    put_rows(start, rows, [(even, offset), (odd, offset)], where, n, n, 3)
    up_body(n, 1, grid, where, coarse, 2, shift, (1, 1), iterate, result, start, one)


def up_last_kernel(n, grids, offsets, where, *refs):
    coarse_own, x_even, x_odd, y_even, y_odd, even, odd = refs[:7]
    shift, iterate_rows, rows, fine_shift, fine_iterate, fine_rows = refs[7:13]
    result, coarse, iterate, start, one, middle, fine_start, fine_one = refs[13:]
    put_frame(coarse, coarse_own, [x_even, x_odd, y_even, y_odd], where, n // 2, 3, 1)
    put_rows(start, rows, [(even, offsets[1]), (odd, offsets[1])], where, n, n, 4)
    put_rows(iterate, iterate_rows, [(even, offsets[2]), (odd, offsets[2])], where, n, n, 2)
    put_rows(fine_start, fine_rows, [(even, offsets[0]), (odd, offsets[0])], where, 2 * n, 2 * n, 2)
    up_body(n, 2, grids[0], where, coarse, 3, shift, (0, 0), iterate, middle, start, one)
    fine_at = (2 * n - 2, 2 * n - 2)
    up_body(2 * n, 0, grids[1], where, middle, 2, fine_shift, fine_at, fine_iterate, result, fine_start, fine_one)


VMEM = pl.BlockSpec(memory_space=pltpu.VMEM)


def call(kernel, operands, outs, scratch, name):
    def run(*refs):
        kernel(spot(), *refs)

    return pl.pallas_call(
        run,
        out_shape=[jax.ShapeDtypeStruct(out, jnp.float32) for out in outs],
        in_specs=[VMEM] * len(operands),
        out_specs=[VMEM] * len(outs),
        scratch_shapes=[pltpu.VMEM(own, jnp.float32) for own in scratch],
        compiler_params=pltpu.CompilerParams(vmem_limit_bytes=12 * 1024 * 1024),
        name=name,
    )(*operands)


def place():
    core, line, far = parity("gy", 1), parity("gx", 1), parity("gx", 2)
    return {"gx": line == 0, "gy": core == 0, "line": line == core, "far": far != core}


def spot():
    core, line, far = parity("gy", 1), parity("gx", 1), parity("gx", 2)
    numbers = [lax.axis_index("gx"), lax.axis_index("gy"), core, line]
    return numbers + [lax.rem(line + core, 2), lax.rem(far + core, 2)]


def grid_of(n):
    return (lax.axis_size("gx") * n, lax.axis_size("gy") * n)


def triangle(columns, n, reach):
    parts = []
    for d, column in enumerate(columns, 1):
        over = (column.shape[0] - n) // 2 - (reach - d)
        parts.append(column[over : column.shape[0] - over])
    return jnp.concatenate(parts, axis=0)


def columns_of(rows, reach):
    width = rows.shape[1]
    return [rows[:, d] for d in range(reach)], [rows[:, width - 1 - d] for d in range(reach)]


def with_rows(strip, rows, tail):
    if rows is None:
        return strip
    rows = rows.reshape(-1, tail[1])
    rows = jnp.pad(rows, ((0, -rows.shape[0] % tail[0]), (0, 0)))
    return jnp.concatenate([strip, rows.reshape((-1,) + tail)], axis=0)


def frame(at, v, reach, beyond=0, blocks=None, rims=None, strips=None):
    n = v.shape[0] - 2 * beyond
    tail = v.shape[-2:]
    own = v[beyond : beyond + n, beyond : beyond + n]
    extra = [blocks, blocks] if rims is None else [rims[-2:], rims[:2]]
    inner = v[:, beyond : beyond + n]
    low, high = strips or (inner[beyond : beyond + reach], inner[beyond + n - reach : beyond + n])
    low, high = with_rows(cells(low), extra[0], tail), with_rows(cells(high), extra[1], tail)
    x_pieces = swap_ends(at, low, high, "gx", 1)
    sides = in_order(at, *x_pieces, "gx")
    strips = [side[: reach * n].reshape((reach, n) + tail) for side in sides]
    rows = jnp.concatenate([strips[0], own, strips[1]], axis=0)
    known = min(reach, n)
    low, high = columns_of(rows, known)
    for d in range(known, reach):
        low.append(v[beyond : beyond + n, beyond + d])
        high.append(v[beyond : beyond + n, beyond + n - 1 - d])
    if blocks is not None or rims is not None:
        sent = extra[0].shape

        def rows_of(side):
            return side[reach * n :].reshape(-1, tail[1])[: sent[0] * sent[1]].reshape(sent)

        extra = jnp.concatenate([rows_of(sides[0]), blocks if rims is None else rims, rows_of(sides[1])], axis=0)
        extra = [extra, extra] if rims is None else [extra[:, -2:], extra[:, :2]]
    low, high = triangle(low, n, reach), triangle(high, n, reach)
    y_pieces = swap_ends(at, with_rows(low, extra[0], tail), with_rows(high, extra[1], tail), "gy", 1)
    return [*x_pieces, *y_pieces]


def by_core(x, swaps):
    lines, blocks = lax.axis_size("gx"), lax.axis_size("gy")
    pairs = []
    for j in range(blocks):
        dist, odd = swaps[j % 2]
        for i in range(lines - dist):
            if (i // dist) % 2 == odd:
                pairs += [(i * blocks + j, (i + dist) * blocks + j), ((i + dist) * blocks + j, i * blocks + j)]
    return lax.ppermute(x, ("gx", "gy"), pairs)


def to_core(x):
    return swap(x, "gy", 1, 0)


def lines_around(near):
    first = by_core(near, [(1, 0), (1, 1)])
    second = by_core(near, [(2, 1), (2, 0)])
    mine = jnp.concatenate([cells(first), cells(second)], axis=0)
    return mine, to_core(mine)


def body(rhs, shift, slots, coarse_inverse):
    at, rhs = lax.optimization_barrier((place(), rhs))
    right = jnp.transpose(rhs, (1, 2, 0, 3))
    n = right.shape[0]
    strips = [jnp.transpose(rows, (1, 2, 0, 3)) for rows in (rhs[:, :HALO], rhs[:, n - HALO :])]
    tail = chans, depth = right.shape[2:]
    half, size = n // 2, n // 4

    def fields(*shapes):
        return [shape + tail for shape in shapes]

    x0, q0, b1, shift_wide, shift_one, shift_two = call(
        functools.partial(down_fine_kernel, n, grid_of(n)),
        [right, *frame(at, right, HALO, 0, shift, None, strips), shift],
        fields((n, n), (n, n), (half, half))
        + [(3 * n, 3 * n, depth), (3 * half, 3 * half, depth), (3 * size, 3 * size, depth)],
        fields((n + 6, n + 6), (n + 4, n + 4), (n + 2, n + 2)),
        "down_fine",
    )
    x1, q1, b2, shift_two = call(
        functools.partial(down_kernel, half, grid_of(half)),
        [b1, *frame(at, b1, HALO, 0, None, shift_two), shift_one, shift_two],
        fields((half, half), (half, half), (size, size)) + [(3 * size + 4, 3 * size + 4, depth)],
        fields((half + 6, half + 6), (half + 4, half + 4), (half + 2, half + 2)),
        "down_middle",
    )

    first_core = at["gy"]
    other = to_core(b2)
    chip = jnp.concatenate([jnp.where(first_core, b2, other), jnp.where(first_core, other, b2)], axis=1)
    mine, others = lines_around(chip)
    near = 2 * size * size
    (mine_near, other_near), (mine_far, other_far) = [
        [v[part].reshape(chip.shape) for v in (mine, others)] for part in (slice(0, near), slice(near, 2 * near))
    ]
    rows = jnp.concatenate(
        [
            jnp.where(at["far"], other_far, mine_far),
            jnp.where(at["line"], other_near, mine_near),
            chip,
            jnp.where(at["line"], mine_near, other_near),
            jnp.where(at["far"], mine_far, other_far),
        ],
        axis=0,
    )
    blocks = lax.axis_size("gy")
    columns = [rows[:, y] for y in range(2 * size)]
    near = jnp.where(first_core, triangle(columns, size, 4), triangle(columns[::-1], size, 4))
    far = [[column[3 + d : -3 - d] for d, column in enumerate(side[:2])] for side in (columns[::-1], columns)]
    far = jnp.where(first_core, *[jnp.concatenate(side, axis=0) for side in far])
    pairs = []
    for j in range(0, blocks - 3, 2):
        pairs += [(j, j + 3), (j + 3, j)]
    x2, q2, b3 = call(
        functools.partial(down_block_kernel, size, grid_of(size)),
        [rows, swap(near, "gy", 1, 1), lax.ppermute(far, "gy", pairs), shift_two],
        fields((size + 2, size + 2), (size + 2, size + 2), (1, 1)),
        fields((size + 8, size + 8), (size + 6, size + 6), (size + 4, size + 4)),
        "down_block",
    )
    b3 = b3[0, 0]

    own = [q0, q1, x1, q2[1:-1, 1:-1]]
    reaches = [2, 4, 2, 3]
    low = jnp.concatenate([cells(q0[:2]), cells(q1), cells(x1[:2]), cells(q2[1:, 1:-1])], axis=0)
    high = jnp.concatenate([cells(q0[-2:]), cells(q1), cells(x1[-2:]), cells(q2[:-1, 1:-1])], axis=0)
    ends = swap_ends(at, low, high, "gx", 1)

    slot = jnp.broadcast_to(slots.astype(jnp.float32), (8, depth))
    shares = lax.all_gather(jnp.concatenate([b3, slot], axis=0)[None], "gy", axis=0, tiled=True)
    ends, shares = lax.optimization_barrier((ends, shares))
    before, after = in_order(at, *ends, "gx")
    around, lows, highs, offsets, done = [], [], [], [0], 0
    for v, reach in zip(own, reaches):
        strip = reach * v.shape[1]
        parts = [side[done : done + strip].reshape((reach,) + v.shape[1:]) for side in (before, after)]
        around.append(jnp.concatenate([parts[0], v, parts[1]], axis=0))
        low, high = columns_of(around[-1], min(reach, v.shape[1]))
        if reach > v.shape[1]:
            low, high = low + [q2[1:-1, -1]], high + [q2[1:-1, 0]]
        lows.append(triangle(low, v.shape[0], reach))
        highs.append(triangle(high, v.shape[0], reach))
        offsets.append(offsets[-1] + lows[-1].shape[0])
        done += strip
    sides = swap_ends(at, jnp.concatenate(lows, axis=0), jnp.concatenate(highs, axis=0), "gy", 1)
    solved = call(
        solve_kernel, [shares, coarse_inverse[0, 0]], [tail], [(chans, blocks * depth)], "solve"
    )[0]
    back = lax.all_gather(solved[None], "gy", axis=0, tiled=True)
    fix = call(pick_kernel, [shares, back], [(6,) + tail], [], "pick")[0]

    x2 = call(
        functools.partial(up_block_kernel, size, grid_of(size), offsets[3]),
        [fix, *lines_around(fix), shift_two, x2, around[3], *sides],
        fields((size + 2, size + 2)),
        fields((5, 5), (size + 6, size + 6), (size + 4, size + 4)),
        "up_block",
    )[0]
    x0 = call(
        functools.partial(up_last_kernel, half, (grid_of(half), grid_of(n)), offsets),
        [x2, *frame(at, x2, 3, 1), *sides, shift_one, around[2], around[1], shift_wide, x0, around[0]],
        fields((n, n)),
        fields(
            (size + 6, size + 6), (half + 4, half + 4), (half + 8, half + 8), (half + 6, half + 6), (half + 4, half + 4),
            (n + 4, n + 4), (n + 2, n + 2),
        ),
        "up_last",
    )[0]
    return jnp.transpose(x0, (2, 0, 1, 3))


def solution(mesh):
    return jax.shard_map(
        body,
        mesh=mesh,
        in_specs=(
            P(None, "gx", "gy", None),
            P("gx", "gy", None),
            P("gx", "gy"),
            P("gx", "gy", None, None),
        ),
        out_specs=P(None, "gx", "gy", None),
        check_vma=False,
    )
```
